32 devices in a mesh: rad: 16 (over z, y, x), lat: 2 (over core).
Axes of the slice: x: 2, y: 2, z: 4, core: 2. Of those that a mesh axis runs over, the one named last changes fastest.
Arguments:
- forcing: float32 [3, 2, 5120, 64], P(None, None, ('rad', 'lat')), may hold values from -6 to 6
- pivots: float32 [5120, 2, 32, 32], P(('rad', 'lat')), may hold values from -1 to 2
- lower: float32 [5120, 1, 32, 32], P(('rad', 'lat')), may hold values from -1 to 2
- upper: float32 [5120, 1, 32, 32], P(('rad', 'lat')), may hold values from -1 to 1.5
- slab_modes: int32 [5], replicated, may hold values from 0 to 511, as said below
- slot_of_column: int32 [5120], replicated, may hold values from 0 to 5119, each once
- legendre: bfloat16 [5, 1024, 768], P(None, None, 'lat'), may hold values from -0.1875 to 0.1875
- cycle_weight: float32 [768], P('lat'), may hold values from 0.5 to 2
- zonal_flow: bfloat16 [64, 768, 1536], P('rad', 'lat'), may hold values from -12 to 12
- inverse_spacing: float32 [64], replicated, may hold values from 0.03 to 0.3
Outputs:
- solved: float32 [3, 2, 5120, 64], P(None, None, ('rad', 'lat'))
- explicit_term: float32 [3, 2, 5120, 64], P(None, None, ('rad', 'lat'))
The draws below stay inside these ranges and needn't reach their ends.
Inputs may be any that keep to these rules, and one draw needn't show every extreme that they name: `slab_modes`: 5 distinct wave numbers below 512, one of them 1024 // 2 - 1. `slot_of_column`: every slot number appears once.
All inputs are finite; a program needn't handle non-finite values.
Results may differ from the reference program's by a relative error of at most 0.0051.
Values may be sent and summed in bfloat16 or wider, within the bound.
A program may use at most 128 MiB of HBM per device.

```python
import math
import jax
import jax.numpy as jnp
from jax import lax

L = 1024
NTH = 768
NPHI = 1536
M = 5
B = 32
K = 5120
R = 64
NB = 2


def pivot_diagonal(key):
    diag_key = jax.random.fold_in(key, 21)
    return jax.random.uniform(diag_key, (K, NB, B, 1), jnp.float32, 0.6, 1.4)


def draw_pivots(key, part):
    diagonal = pivot_diagonal(key)
    key = jax.random.fold_in(key, 11)
    spread = jnp.clip(jax.random.normal(key, (K, NB, B, B), jnp.float32), -4.0, 4.0) * (0.35 / math.sqrt(B))
    return jnp.eye(B, dtype=jnp.float32) * diagonal + spread


def draw_lower(key, part):
    diagonal = pivot_diagonal(key)[:, 1:]
    key = jax.random.fold_in(key, 14)
    rate_key, noise_key = jax.random.split(key)
    rate = jax.random.uniform(rate_key, (K, NB - 1, B, 1), jnp.float32, 0.6, 0.85)
    noise = jnp.clip(jax.random.normal(noise_key, (K, NB - 1, B, B), jnp.float32), -4.0, 4.0) * (0.2 / math.sqrt(B))
    return jnp.eye(B, dtype=jnp.float32) * (rate / diagonal) + noise


def draw_upper(key, part):
    key = jax.random.fold_in(key, 15)
    rate_key, noise_key = jax.random.split(key)
    rate = jax.random.uniform(rate_key, (K, NB - 1, B, 1), jnp.float32, 0.6, 0.85)
    noise = jnp.clip(jax.random.normal(noise_key, (K, NB - 1, B, B), jnp.float32), -4.0, 4.0) * (0.2 / math.sqrt(B))
    return jnp.eye(B, dtype=jnp.float32) * rate + noise


def draw_slab_modes(key, part):
    key = jax.random.fold_in(key, 12)
    pick_key, order_key = jax.random.split(key)
    others = jax.random.permutation(pick_key, L // 2 - 1)[:M - 1].astype(jnp.int32)
    top = jnp.full((1,), L // 2 - 1, jnp.int32)
    chosen = jnp.concatenate([others, top], 0)
    return jax.random.permutation(order_key, chosen).astype(jnp.int32)


def draw_zonal_flow(key, part):
    key = jax.random.fold_in(key, 13)
    mean_key, noise_key = jax.random.split(key)
    zonal_mean = jnp.clip(jax.random.normal(mean_key, (R, NTH, 1), jnp.float32), -4.0, 4.0)
    noise = jnp.clip(jax.random.normal(noise_key, (R, NTH, NPHI), jnp.float32), -4.0, 4.0)
    return (zonal_mean + 2.0 * noise).astype(jnp.bfloat16)


def levels(key, extent, cuts, low, largest):
    loudness = 1.0
    for axis_at, parts in cuts:
        draws = jax.random.uniform(jax.random.fold_in(jax.random.fold_in(key, 6), axis_at), (parts,), jnp.float32, low / len(cuts), largest / len(cuts))
        loudness = loudness * jnp.repeat(jnp.exp(draws), extent[axis_at] // parts).reshape((-1,) + (1,) * (len(extent) - 1 - axis_at))
    return loudness


def normal_values(stream_key, dims, deviation, most, shards=(), kind=jnp.bfloat16):
    gain = levels(stream_key, dims, shards, -0.22, 0.18) if shards else 1.0
    drawn = jax.random.normal(stream_key, dims, jnp.float32) * deviation * gain
    return jnp.minimum(jnp.maximum(drawn, -most), most).astype(kind)


def setup_inputs(seed: int = 0) -> dict:
    key_of = jax.random.split(jax.random.key(seed), 11)
    return {
        "forcing": normal_values(key_of[0], (3, 2, K, R), 1.0, 6.0, ((2, 32),), jnp.float32),
        "pivots": draw_pivots(jax.random.fold_in(key_of[10], 71), 0),
        "lower": draw_lower(jax.random.fold_in(key_of[10], 71), 0),
        "upper": draw_upper(jax.random.fold_in(key_of[10], 71), 0),
        "slab_modes": draw_slab_modes(jax.random.fold_in(key_of[10], 71), 0),
        "slot_of_column": jax.random.permutation(key_of[5], K).astype(jnp.int32),
        "legendre": normal_values(key_of[6], (M, L, NTH), L ** -0.5, 0.1875, ((2, 2),)),
        "cycle_weight": jnp.clip(jnp.exp(math.log(2.0) - 1.3862944 * jax.random.uniform(key_of[7], (NTH,), jnp.float32) ** levels(key_of[7], (NTH,), ((0, 2),), -0.2, 0.2)), 0.5, 2.0),
        "zonal_flow": draw_zonal_flow(jax.random.fold_in(key_of[10], 71), 0),
        "inverse_spacing": jnp.clip(jnp.exp(jax.random.uniform(key_of[9], (R,), jnp.float32, math.log(0.03), math.log(0.3))), 0.03, 0.3),
    }


def radial_solve(forcing, pivots, lower, upper):
    slot_count = forcing.shape[2]
    block_count = pivots.shape[1]
    block_size = pivots.shape[2]
    highest = lax.Precision.HIGHEST
    blocks = jnp.moveaxis(forcing.reshape(3, 2, slot_count, block_count, block_size), 3, 0)

    def apply_block(matrix, vector):
        return jnp.einsum("kij,fckj->fcki", matrix, vector, precision=highest)

    leading = apply_block(pivots[:, 0], blocks[0])

    def descend(carry, element):
        pivot_block, lower_block, rhs_block = element
        advanced = apply_block(pivot_block, rhs_block - apply_block(lower_block, carry))
        return advanced, advanced

    _, trailing = lax.scan(descend, leading, (jnp.moveaxis(pivots[:, 1:], 1, 0), jnp.moveaxis(lower, 1, 0), blocks[1:]))
    forward = jnp.concatenate([leading[None], trailing], 0)
    final_block = forward[-1]

    def up_step(carry, element):
        upper_block, forward_block = element
        current = forward_block - apply_block(upper_block, carry)
        return current, current

    _, earlier = lax.scan(up_step, final_block, (jnp.moveaxis(upper, 1, 0), forward[:-1]), reverse=True)
    result = jnp.concatenate([earlier, final_block[None]], 0)
    return jnp.moveaxis(result, 0, 3).reshape(3, 2, slot_count, block_count * block_size)


def phi_tables(slab_modes, phi_count, degree_count):
    columns = jnp.arange(phi_count, dtype=jnp.int32)
    residues = (slab_modes[:, None] * columns[None, :]) % phi_count
    angles = residues.astype(jnp.float32) * (2.0 * math.pi / phi_count)
    factor = slab_modes.astype(jnp.float32)[:, None] * (2.0 / degree_count)
    slope_table = jnp.concatenate([-factor * jnp.sin(angles), -factor * jnp.cos(angles)], 0).astype(jnp.bfloat16)
    back_table = (jnp.concatenate([jnp.cos(angles), -jnp.sin(angles)], 0) * (2.0 / phi_count)).astype(jnp.bfloat16)
    return slope_table, back_table


def stencil(padded, center, spacing):
    width = center.shape[3]
    differences = padded[..., 0:width] - 8.0 * padded[..., 1:width + 1] + 8.0 * padded[..., 3:width + 3] - padded[..., 4:width + 4]
    return center + spacing * differences


def reference(forcing, pivots, lower, upper, slab_modes, slot_of_column, legendre, cycle_weight, zonal_flow, inverse_spacing):
    highest = lax.Precision.HIGHEST
    solved = radial_solve(forcing, pivots, lower, upper)
    slot_count = slot_of_column.shape[0]
    positions = jnp.arange(slot_count, dtype=jnp.int32)
    inverse = jnp.zeros((slot_count,), jnp.int32).at[slot_of_column].set(positions)
    coeffs = jnp.take(solved.astype(jnp.bfloat16), inverse, axis=2).reshape(3, 2, M, L, R)
    allowed = jnp.arange(L, dtype=jnp.int32)[None, :] >= slab_modes[:, None]
    coeffs = coeffs * allowed.astype(jnp.bfloat16)[None, None, :, :, None]
    slope_table, back_table = phi_tables(slab_modes, NPHI, L)
    slope32 = slope_table.astype(jnp.float32)
    back32 = back_table.astype(jnp.float32)
    legendre32 = legendre.astype(jnp.float32)

    def one_level(element):
        level_coeffs, level_flow = element
        spectral = jnp.einsum("fcml,mlt->ftcm", level_coeffs.astype(jnp.float32), legendre32, precision=highest)
        spectral = lax.optimization_barrier(spectral.astype(jnp.bfloat16)).astype(jnp.float32)
        spectral = spectral.reshape(3, NTH, 2 * M)
        gradient = jnp.einsum("ftk,kp->ftp", spectral, slope32, precision=highest)
        product = (gradient * level_flow.astype(jnp.float32)[None]).astype(jnp.bfloat16)
        product = lax.optimization_barrier(product).astype(jnp.float32)
        modal = jnp.einsum("ftp,kp->ftk", product, back32, precision=highest)
        weighted = (modal.reshape(3, NTH, 2, M) * cycle_weight[None, :, None, None]).astype(jnp.bfloat16)
        weighted = lax.optimization_barrier(weighted).astype(jnp.float32)
        return jnp.einsum("ftcm,mlt->fcml", weighted, legendre32, precision=highest)

    advection = lax.map(one_level, (jnp.moveaxis(coeffs, 4, 0), zonal_flow))
    advection = jnp.moveaxis(advection, 0, 4) * allowed.astype(jnp.float32)[None, None, :, :, None]
    advection = advection.reshape(3, 2, slot_count, R)
    padded = jnp.pad(advection, ((0, 0), (0, 0), (0, 0), (2, 2)))
    explicit = stencil(padded, advection, inverse_spacing)
    explicit_term = jnp.take(explicit, slot_of_column, axis=2)
    return solved, explicit_term
```

```python
import functools
import math

import jax
import jax.numpy as jnp
from jax import lax
from jax.experimental import pallas as pl
from jax.experimental.pallas import tpu as pltpu
from jax.sharding import PartitionSpec as P

LANES = 128
LOW = 256
MESH = pl.DeviceIdType.MESH
VMEM = pl.BlockSpec(memory_space=pltpu.VMEM)
SMEM = pl.BlockSpec(memory_space=pltpu.SMEM)
F32 = jnp.float32
BF16 = jnp.bfloat16
ROOM = 48 * 1024 * 1024


def params(room=ROOM, **more):
    return pltpu.CompilerParams(vmem_limit_bytes=room, **more)


def phi_tables(slab_modes, phi_count, degree_count):
    columns = jnp.arange(phi_count, dtype=jnp.int32)
    residues = slab_modes[:, None] * columns[None, :] % phi_count
    angles = residues.astype(jnp.float32) * (2.0 * math.pi / phi_count)
    factor = slab_modes.astype(jnp.float32)[:, None] * (2.0 / degree_count)
    slope_table = jnp.concatenate([-factor * jnp.sin(angles), -factor * jnp.cos(angles)], 0).astype(
        jnp.bfloat16
    )
    back_table = (
        jnp.concatenate([jnp.cos(angles), -jnp.sin(angles)], 0) * (2.0 / phi_count)
    ).astype(jnp.bfloat16)
    return (slope_table, back_table)


class Blocks:
    def __init__(self, columns, values):
        self.columns, self.values = columns, values
        self.full, self.tail = divmod(columns, LANES)
        self.groups = values // 8
        self.packed = self.full > 0 and 0 < self.tail and self.tail * self.groups <= LANES
        self.packed = self.packed and LANES % self.tail == 0
        self.rows = self.full * values + 8 if self.packed else -(-columns // LANES) * values
        self.rows_held = -(-self.rows // 16) * 16
        self.share = LANES // self.tail if self.packed else 1

    def pack(self, value):
        parts = [value[:, i * LANES : (i + 1) * LANES] for i in range(self.full)]
        rest = value[:, self.full * LANES :]
        if self.packed:
            pieces = [rest[8 * g : 8 * g + 8] for g in range(self.groups)]
            spare = LANES - self.tail * self.groups
            if spare:
                pieces.append(jnp.zeros((8, spare), value.dtype))
            parts.append(jnp.concatenate(pieces, 1))
        elif self.tail:
            parts.append(
                jnp.concatenate([rest, jnp.zeros((self.values, LANES - self.tail), value.dtype)], 1)
            )
        if self.rows_held > self.rows:
            parts.append(jnp.zeros((self.rows_held - self.rows, LANES), value.dtype))
        return jnp.concatenate(parts, 0)

    def order(self, per_column, devices):
        table = per_column.reshape(devices, self.columns)
        whole = self.full if self.packed else -(-self.columns // LANES)
        if not self.packed and self.tail:
            table = jnp.pad(table, ((0, 0), (0, whole * LANES - self.columns)), constant_values=-1)
        parts = [table[:, : whole * LANES].reshape(-1)]
        if self.packed:
            parts.append(table[:, whole * LANES :].reshape(-1))
        return jnp.concatenate(parts)


def solve_kernel(blocks, ranks, forcing, pivots, lower, upper, solved, send, stage):
    items, depth, columns = forcing.shape
    count, size = pivots.shape[0], pivots.shape[1]
    levels = depth // ranks

    def apply_block(matrix, at, vectors):
        pieces = [[] for _ in vectors]
        for i in range(0, size, 8):
            rows = matrix[at, i : i + 8]
            for item, vector in enumerate(vectors):
                pieces[item].append(jnp.sum(rows * vector[None], axis=1))
        return [jnp.concatenate(p, 0) for p in pieces]

    def span(k):
        return pl.ds(k * size if isinstance(k, int) else pl.multiple_of(k * size, size), size)

    first = apply_block(pivots, 0, [forcing[item, span(0)] for item in range(items)])
    for item in range(items):
        solved[item, span(0)] = first[item]

    def descend(k, carry):
        drop = apply_block(lower, k - 1, carry)
        rest = [forcing[item, span(k)] - drop[item] for item in range(items)]
        now = apply_block(pivots, k, rest)
        for item in range(items):
            solved[item, span(k)] = now[item]
        return tuple(now)

    last = tuple(first)
    for k in range(1, count) if count <= 2 else ():
        last = descend(k, last)
    if count > 2:
        last = lax.fori_loop(1, count, descend, last)

    def up_step(step, carry):
        k = count - 2 - step
        drop = apply_block(upper, k, carry)
        now = [solved[item, span(k)] - drop[item] for item in range(items)]
        for item in range(items):
            solved[item, span(k)] = now[item]
        return tuple(now)

    if count <= 2:
        for step in range(count - 1):
            last = up_step(step, last)
    else:
        lax.fori_loop(0, count - 1, up_step, last)

    for rank in range(ranks):
        for item in range(items):
            stage[rank, item * levels : (item + 1) * levels, :] = solved[
                item, rank * levels : (rank + 1) * levels, :
            ]

    def give(rank, _):
        send[rank] = blocks.pack(stage[rank]).astype(BF16)
        return 0

    lax.fori_loop(0, ranks, give, 0)


def wave_kernel(modes, slope, back, zonal, out):
    levels = zonal.shape[0]
    parts = out.shape[0]
    s, b = slope[...].astype(F32), back[...].astype(F32)
    rows = []
    for e in range(2):
        for i in range(modes):
            for j in range(modes):
                for c in range(2):
                    a = c if e == 0 else 1 - c
                    rows.append(
                        s[a * modes + i : a * modes + i + 1] * b[c * modes + j : c * modes + j + 1]
                    )
    total = len(rows)
    spare = -total % 8
    table = jnp.concatenate(rows + [jnp.zeros((spare, s.shape[1]), F32)] * (spare > 0), 0)
    high = table.astype(BF16)
    low = (table - high.astype(F32)).astype(BF16)
    for r in range(levels):
        flow = zonal[r]
        dims = (((1,), (1,)), ((), ()))
        value = lax.dot_general(high, flow, dims, preferred_element_type=F32)
        value = value + lax.dot_general(low, flow, dims, preferred_element_type=F32)
        for part in range(parts):
            out[part, pl.ds(r, total, stride=levels), :] = value[
                :total, part * LANES : (part + 1) * LANES
            ]


def legendre_kernel(
    blocks, devices, ranks, modes_ref, slots, message, legendre, weight, waves, out,
    hot, spread, spectral, turned
):
    values = blocks.values
    modes, degrees, cycles = legendre.shape
    chunks = degrees // LOW
    total = slots.shape[1]
    whole = blocks.full if blocks.packed else -(-blocks.columns // LANES)
    main = devices * whole * LANES
    high_count = modes * chunks

    def side(at):
        return pl.ds(pl.multiple_of(at * LANES, LANES), LANES)

    def scatter(at, value):
        slot = slots[:, side(at)]
        high, low = slot // LOW, slot % LOW
        rows = lax.broadcasted_iota(jnp.int32, (LOW, LANES), 0)
        hot[:, side(at)] = jnp.where(rows == low, 1.0, 0.0).astype(BF16)
        for h in range(0, high_count, 2):
            pair = [jnp.where(high == h + n, value, 0.0) for n in range(2)]
            spread[h * values : (h + 2) * values, side(at)] = jnp.concatenate(pair, 0).astype(BF16)

    def main_step(device, _):
        block = message[device].astype(F32)
        for n in range(whole):
            scatter(device * whole + n, block[n * values : (n + 1) * values])
        return 0

    lax.fori_loop(0, devices, main_step, 0)

    if blocks.packed:
        share, tail = blocks.share, blocks.tail
        base = blocks.full * values

        def tail_step(group, _):
            held = [
                message[group * share + d].astype(F32)[base : base + 8] for d in range(share)
            ]
            pieces = [
                jnp.concatenate([h[:, g * tail : (g + 1) * tail] for h in held], 1)
                for g in range(blocks.groups)
            ]
            scatter(devices * whole + group, jnp.concatenate(pieces, 0))
            return 0

        lax.fori_loop(0, devices // share, tail_step, 0)

    coeffs = lax.dot_general(
        spread[...], hot[...], (((1,), (1,)), ((), ())), preferred_element_type=F32
    )
    lane = lax.broadcasted_iota(jnp.int32, (values, LOW), 1)

    def allowed(i, n):
        return lane + n * LOW >= modes_ref[i]

    for i in range(modes):
        rows = []
        for n in range(chunks):
            at = (i * chunks + n) * values
            rows.append(jnp.where(allowed(i, n), coeffs[at : at + values], 0.0).astype(BF16))
        value = jnp.dot(jnp.concatenate(rows, 1), legendre[i], preferred_element_type=F32)
        value = value.astype(BF16).astype(F32)
        spectral[i] = value
        for f in range(values // 8):
            block = value[f * 8 : f * 8 + 8]
            turned[i, f * 8 : f * 8 + 8] = jnp.concatenate([block[4:8], block[0:4]], 0)

    sums = []
    for j in range(modes):
        fields = []
        for f in range(values // 8):
            parts = []
            for part in range(cycles // LANES):
                acc = None
                for e, source in enumerate((spectral, turned)):
                    for i in range(modes):
                        at = ((e * modes + i) * modes + j) * 8
                        term = (
                            source[i, f * 8 : f * 8 + 8, part * LANES : (part + 1) * LANES]
                            * waves[part, at : at + 8, :]
                        )
                        acc = term if acc is None else acc + term
                parts.append(acc)
            fields.append(jnp.concatenate(parts, 1))
        sums.append((jnp.concatenate(fields, 0) * weight[...]).astype(BF16))

    pieces_high, pieces_low = [], []
    for i in range(modes):
        for n in range(chunks):
            value = lax.dot_general(
                sums[i], legendre[i, n * LOW : (n + 1) * LOW, :], (((1,), (1,)), ((), ())),
                preferred_element_type=F32,
            )
            value = jnp.where(allowed(i, n), value, 0.0)
            high = value.astype(BF16).astype(F32)
            pieces_high.append(high)
            pieces_low.append(value - high)
    both = jnp.concatenate(pieces_high + pieces_low, 0).astype(BF16)
    split = high_count * values

    def collect(at):
        value = jnp.dot(both, hot[:, side(at)], preferred_element_type=F32)
        high = slots[:, side(at)] // LOW
        acc = jnp.zeros((values, LANES), F32)
        for h in range(high_count):
            term = value[h * values : (h + 1) * values]
            term = term + value[split + h * values : split + (h + 1) * values]
            acc = acc + jnp.where(high == h, term, 0.0)
        return acc

    def back_step(device, _):
        for n in range(whole):
            out[device, n * values : (n + 1) * values, :] = collect(device * whole + n)
        return 0

    lax.fori_loop(0, devices, back_step, 0)

    if blocks.packed:

        def tail_back(group, _):
            value = collect(devices * whole + group)
            for d in range(share):
                pieces = [
                    value[g * 8 : g * 8 + 8, d * tail : (d + 1) * tail]
                    for g in range(blocks.groups)
                ]
                spare = LANES - tail * blocks.groups
                if spare:
                    pieces.append(jnp.zeros((8, spare), F32))
                out[group * share + d, base : base + 8, :] = jnp.concatenate(pieces, 1)
            return 0

        lax.fori_loop(0, devices // share, tail_back, 0)


def meet(ranks, me, other):
    barrier = pltpu.get_barrier_semaphore()

    def hello(d, _):
        pl.semaphore_signal(
            barrier, inc=1, device_id=(lax.rem(me + d, ranks), 1 - other), device_id_type=MESH
        )
        return 0

    def peers(d, _):
        pl.semaphore_signal(
            barrier, inc=1, device_id=(lax.rem(me + d, ranks), other), device_id_type=MESH
        )
        return 0

    hello(0, 0)
    lax.fori_loop(1, ranks, peers, 0)
    pl.semaphore_wait(barrier, ranks)


def forward_kernel(ranks, send, out, send_sem, recv_sem, pass_sem, got_sem, own_sem):
    me, lat = lax.axis_index("rad"), lax.axis_index("lat")
    meet(ranks, me, lat)

    def to_rank(rank, source):
        return pltpu.make_async_remote_copy(
            src_ref=send.at[rank],
            dst_ref=out.at[source, lat],
            send_sem=send_sem.at[rank],
            recv_sem=recv_sem.at[source],
            device_id=(rank, lat),
            device_id_type=MESH,
        )

    def to_pair(ref, source, half):
        return pltpu.make_async_remote_copy(
            src_ref=ref,
            dst_ref=out.at[source, half],
            send_sem=pass_sem.at[source],
            recv_sem=got_sem.at[source],
            device_id=(me, 1 - lat),
            device_id_type=MESH,
        )

    def begin(d, _):
        to_rank(lax.rem(me + d, ranks), me).start()
        return 0

    lax.fori_loop(1, ranks, begin, 0)
    to_pair(send.at[me], me, lat).start()
    own = pltpu.make_async_copy(send.at[me], out.at[me, lat], own_sem)
    own.start()

    def hand_on(d, _):
        source = lax.rem(me + ranks - d, ranks)
        to_rank(source, source).wait_recv()
        to_pair(out.at[source, lat], source, lat).start()
        return 0

    lax.fori_loop(1, ranks, hand_on, 0)
    own.wait()

    def finish(source, _):
        to_pair(out.at[source, lat], source, 1 - lat).wait()
        return 0

    lax.fori_loop(0, ranks, finish, 0)

    def sent(d, _):
        to_rank(lax.rem(me + d, ranks), me).wait_send()
        return 0

    lax.fori_loop(1, ranks, sent, 0)


def backward_kernel(
    ranks, partial, out, other, total, send_sem, recv_sem, pass_sem, got_sem
):
    me, lat = lax.axis_index("rad"), lax.axis_index("lat")
    meet(ranks, me, lat)

    def to_pair(rank):
        return pltpu.make_async_remote_copy(
            src_ref=partial.at[rank, 1 - lat],
            dst_ref=other.at[rank],
            send_sem=pass_sem.at[rank],
            recv_sem=got_sem.at[rank],
            device_id=(me, 1 - lat),
            device_id_type=MESH,
        )

    def to_rank(rank, source):
        return pltpu.make_async_remote_copy(
            src_ref=total.at[rank],
            dst_ref=out.at[source],
            send_sem=send_sem.at[rank],
            recv_sem=recv_sem.at[source],
            device_id=(rank, lat),
            device_id_type=MESH,
        )

    def begin(d, _):
        to_pair(lax.rem(me + d, ranks)).start()
        return 0

    lax.fori_loop(1, ranks + 1, begin, 0)

    def add(d, _):
        rank = lax.rem(me + d, ranks)
        to_pair(rank).wait_recv()
        total[rank] = (partial[rank, lat] + other[rank]).astype(total.dtype)
        to_rank(rank, me).start()
        return 0

    lax.fori_loop(1, ranks, add, 0)
    to_pair(me).wait_recv()
    out[me] = (partial[me, lat] + other[me]).astype(out.dtype)

    def finish(d, _):
        source = lax.rem(me + ranks - d, ranks)
        to_rank(source, source).wait_recv()
        return 0

    lax.fori_loop(1, ranks, finish, 0)

    def sent(d, _):
        to_rank(lax.rem(me + d, ranks), me).wait_send()
        return 0

    lax.fori_loop(1, ranks, sent, 0)

    def passed(rank, _):
        to_pair(rank).wait_send()
        return 0

    lax.fori_loop(0, ranks, passed, 0)


def stencil_kernel(blocks, ranks, spacing, got, out, held):
    items, depth, columns = out.shape
    levels = depth // ranks
    values = blocks.values
    edge = 8
    held[:, 0:edge, :] = jnp.zeros((items, edge, columns), F32)
    held[:, edge + depth : 2 * edge + depth, :] = jnp.zeros((items, edge, columns), F32)

    for rank in range(ranks):
        value = got[rank].astype(F32)
        parts = [value[n * values : (n + 1) * values] for n in range(blocks.full)]
        if blocks.packed:
            base = blocks.full * values
            parts.append(
                jnp.concatenate(
                    [
                        value[base : base + 8, g * blocks.tail : (g + 1) * blocks.tail]
                        for g in range(blocks.groups)
                    ],
                    0,
                )
            )
        elif blocks.tail:
            base = blocks.full * values
            parts.append(value[base : base + values, : blocks.tail])
        at = edge + rank * levels
        lane = 0
        for part in parts:
            width = part.shape[1]
            for item in range(items):
                held[item, at : at + levels, lane : lane + width] = part[
                    item * levels : (item + 1) * levels
                ]
            lane += width

    factor = spacing[...]
    for item in range(items):
        def shifted(n):
            return held[item, edge + n : edge + n + depth, :]

        slope = shifted(-2) - 8.0 * shifted(-1) + 8.0 * shifted(1) - shifted(2)
        out[item] = shifted(0) + factor * slope


def body(
    forcing,
    pivots,
    lower,
    upper,
    slab_modes,
    slot_of_column,
    legendre,
    cycle_weight,
    zonal_flow,
    inverse_spacing,
):
    ranks, halves = lax.axis_size("rad"), lax.axis_size("lat")
    devices = ranks * halves
    columns, depth = forcing.shape[2], forcing.shape[3]
    modes, degrees, cycles = legendre.shape
    levels, _, phi_count = zonal_flow.shape
    items = 6
    values = items * levels
    blocks = Blocks(columns, values)
    rows = blocks.rows_held

    right = forcing.transpose(0, 1, 3, 2).reshape(items, depth, columns)
    solved, send = pl.pallas_call(
        functools.partial(solve_kernel, blocks, ranks),
        out_shape=(
            jax.ShapeDtypeStruct((items, depth, columns), F32),
            jax.ShapeDtypeStruct((ranks, rows, LANES), BF16),
        ),
        in_specs=[VMEM] * 4,
        out_specs=(VMEM, VMEM),
        scratch_shapes=[pltpu.VMEM((ranks, values, columns), F32)],
        compiler_params=params(),
        name="solve",
    )(right, *(m.transpose(1, 2, 3, 0) for m in (pivots, lower, upper)))

    got = pl.pallas_call(
        functools.partial(forward_kernel, ranks),
        out_shape=jax.ShapeDtypeStruct((ranks, halves, rows, LANES), BF16),
        in_specs=[VMEM],
        out_specs=VMEM,
        scratch_shapes=[pltpu.SemaphoreType.DMA((ranks,))] * 4 + [pltpu.SemaphoreType.DMA],
        compiler_params=params(collective_id=0, has_side_effects=True),
        name="forward",
    )(send)

    slope_table, back_table = phi_tables(slab_modes, phi_count, degrees)
    waves = pl.pallas_call(
        functools.partial(wave_kernel, modes),
        out_shape=jax.ShapeDtypeStruct(
            (cycles // LANES, 4 * modes * modes * levels, LANES), F32
        ),
        in_specs=[VMEM] * 3,
        out_specs=VMEM,
        compiler_params=params(),
        name="waves",
    )(slope_table, back_table, zonal_flow)

    slots = blocks.order(slot_of_column, devices)[None]
    total = slots.shape[1]
    high_count = modes * (degrees // LOW)
    partial = pl.pallas_call(
        functools.partial(legendre_kernel, blocks, devices, ranks),
        out_shape=jax.ShapeDtypeStruct((devices, rows, LANES), F32),
        in_specs=[SMEM] + [VMEM] * 5,
        out_specs=VMEM,
        scratch_shapes=[
            pltpu.VMEM((LOW, total), BF16),
            pltpu.VMEM((high_count * values, total), BF16),
            pltpu.VMEM((modes, values, cycles), F32),
            pltpu.VMEM((modes, values, cycles), F32),
        ],
        compiler_params=params(ROOM if total <= 8192 else 60 * 1024 * 1024),
        name="legendre",
    )(slab_modes, slots, got.reshape(devices, rows, LANES), legendre, cycle_weight[None], waves)

    back = pl.pallas_call(
        functools.partial(backward_kernel, ranks),
        out_shape=jax.ShapeDtypeStruct((ranks, rows, LANES), F32),
        in_specs=[VMEM],
        out_specs=VMEM,
        scratch_shapes=[
            pltpu.VMEM((ranks, rows, LANES), F32),
            pltpu.VMEM((ranks, rows, LANES), F32),
        ]
        + [pltpu.SemaphoreType.DMA((ranks,))] * 4,
        compiler_params=params(collective_id=1, has_side_effects=True),
        name="backward",
    )(partial.reshape(ranks, halves, rows, LANES))

    explicit = pl.pallas_call(
        functools.partial(stencil_kernel, blocks, ranks),
        out_shape=jax.ShapeDtypeStruct((items, depth, columns), F32),
        in_specs=[VMEM] * 2,
        out_specs=VMEM,
        scratch_shapes=[pltpu.VMEM((items, depth + 16, columns), F32)],
        compiler_params=params(),
        name="stencil",
    )(inverse_spacing[:, None], back)

    def placed(value):
        return value.reshape(3, 2, depth, columns).transpose(0, 1, 3, 2)

    return (placed(solved), placed(explicit))


def solution(mesh):
    placed = (
        P(None, None, ("rad", "lat"), None),
        P(("rad", "lat"), None, None, None),
        P(("rad", "lat"), None, None, None),
        P(("rad", "lat"), None, None, None),
        P(),
        P(),
        P(None, None, "lat"),
        P("lat"),
        P("rad", "lat", None),
        P(),
    )
    return jax.shard_map(
        body,
        mesh=mesh,
        in_specs=placed,
        out_specs=(P(None, None, ("rad", "lat"), None), P(None, None, ("rad", "lat"), None)),
        check_vma=False,
    )
```

```python
import functools
import math

import jax
import jax.numpy as jnp
from jax import lax
from jax.experimental import pallas as pl
from jax.experimental.pallas import tpu as pltpu
from jax.sharding import PartitionSpec as P

LANES = 128
SHIFT = 8
LOW = 1 << SHIFT
MESH = pl.DeviceIdType.MESH
VMEM = pl.BlockSpec(memory_space=pltpu.VMEM)
SMEM = pl.BlockSpec(memory_space=pltpu.SMEM)
ANY = pl.BlockSpec(memory_space=pl.ANY)
F32 = jnp.float32
BF16 = jnp.bfloat16
ROOM = 60 * 1024 * 1024


class Blocks:
    def __init__(self, columns, values, ranks):
        self.columns, self.values, self.ranks = columns, values, ranks
        self.full, self.tail = divmod(columns, LANES)
        self.groups = values // 8
        self.slot = 8
        while self.slot < self.tail:
            self.slot *= 2
        assert self.full <= 1 and self.slot * self.groups <= LANES
        self.base = self.full * values
        self.rows = -(-(self.base + 8) // 16) * 16
        self.share = LANES // self.slot
        self.main = ranks * self.full * LANES
        self.half = self.main + ranks * self.slot

    def join(self, main, tail):
        parts = ([main] if self.full else []) + [tail]
        spare = self.rows - self.base - 8
        if spare:
            parts.append(jnp.zeros((spare, LANES), tail.dtype))
        return jnp.concatenate(parts, 0)

    def lanes(self, pieces):
        parts = []
        for piece in pieces:
            parts.append(piece)
            if piece.shape[1] < self.slot:
                parts.append(jnp.zeros((8, self.slot - piece.shape[1]), piece.dtype))
        spare = LANES - self.slot * len(pieces)
        if spare:
            parts.append(jnp.zeros((8, spare), pieces[0].dtype))
        return jnp.concatenate(parts, 1)

    def pack(self, value):
        rest = value[:, self.full * LANES :]
        tail = self.lanes([rest[8 * g : 8 * g + 8] for g in range(self.groups)])
        return self.join(value[:, : self.full * LANES], tail)

    def order(self, per_column, halves):
        table = per_column.reshape(self.ranks, halves, self.columns).transpose(1, 0, 2)
        main = table[:, :, : self.full * LANES].reshape(halves, self.main)
        tail = table[:, :, self.full * LANES :]
        tail = jnp.pad(
            tail, ((0, 0), (0, 0), (0, self.slot - self.tail)), constant_values=-1
        ).reshape(halves, self.ranks * self.slot)
        return jnp.concatenate([main, tail], 1).reshape(1, halves * self.half)


def sublane_sums(values):
    row = lax.broadcasted_iota(jnp.int32, values[0].shape, 0)
    step = 1
    while len(values) > 1:
        keep = (row & step) == 0
        merged = []
        for first, second in zip(values[0::2], values[1::2]):
            straight = jnp.where(keep, first, second)
            crossed = jnp.where(keep, second, first)
            merged.append(straight + pltpu.roll(crossed, step, 0))
        values, step = merged, step * 2
    return values[0]


def kernel(
    blocks, halves, modes_ref, slots, spacing, weight, forcing_hbm, pivots_hbm, lower_hbm,
    upper_hbm, zonal_hbm, legendre_hbm, solved_hbm, out,
    forcing, pivots, lower, upper, zonal, legendre, solved, stage, send, message, hot, spread,
    waves, spectral, turned, tails, give, other, total, back, held,
    load_sem, solved_sem, send_sem, recv_sem, pass_sem, got_sem,
    send2_sem, recv2_sem, pass2_sem, got2_sem,
):
    me, lat = lax.axis_index("rad"), lax.axis_index("lat")
    ranks, values, base = blocks.ranks, blocks.values, blocks.base
    items, depth, columns = forcing.shape
    count, size = pivots.shape[0], pivots.shape[1]
    levels = depth // ranks
    modes, degrees, cycles = legendre.shape
    phi_count = zonal.shape[2]
    chunks = degrees // LOW
    high_count = modes * chunks
    fields = values // 8

    loads = [
        pltpu.make_async_copy(source, target, load_sem.at[n])
        for n, (source, target) in enumerate(
            (
                (forcing_hbm, forcing), (pivots_hbm, pivots), (lower_hbm, lower),
                (upper_hbm, upper), (zonal_hbm, zonal), (legendre_hbm, legendre),
            )
        )
    ]
    for load in loads:
        load.start()

    barrier = pltpu.get_barrier_semaphore()
    pl.semaphore_signal(barrier, inc=1, device_id=(me, 1 - lat), device_id_type=MESH)

    def hello(d, _):
        rank = lax.rem(me + d, ranks)
        pl.semaphore_signal(barrier, inc=1, device_id=(rank, lat), device_id_type=MESH)
        return 0

    lax.fori_loop(1, ranks, hello, 0)

    def to_rank(rank, source):
        return pltpu.make_async_remote_copy(
            src_ref=send.at[rank], dst_ref=message.at[lat, source],
            send_sem=send_sem.at[rank], recv_sem=recv_sem.at[source],
            device_id=(rank, lat), device_id_type=MESH,
        )

    def to_pair(source, half):
        return pltpu.make_async_remote_copy(
            src_ref=message.at[lat, source], dst_ref=message.at[half, source],
            send_sem=pass_sem.at[source], recv_sem=got_sem.at[source],
            device_id=(me, 1 - lat), device_id_type=MESH,
        )

    def apply_block(matrix, at, vectors):
        pieces = [[] for _ in vectors]
        for i in range(0, size, 8):
            for item, vector in enumerate(vectors):
                sums = []
                for n in range(8):
                    acc = matrix[at, i + n, 0:8] * vector[0:8]
                    for j in range(8, size, 8):
                        acc = acc + matrix[at, i + n, j : j + 8] * vector[j : j + 8]
                    sums.append(acc)
                pieces[item].append(sublane_sums(sums))
        return [jnp.concatenate(p, 0) for p in pieces]

    def span(k):
        return pl.ds(k * size if isinstance(k, int) else pl.multiple_of(k * size, size), size)

    per_block = size // levels

    def emit(k, vectors):
        for u in range(per_block):
            for item in range(items):
                stage[k * per_block + u, item * levels : (item + 1) * levels, :] = vectors[item][
                    u * levels : (u + 1) * levels
                ]

        def give_one(u, _):
            rank = k * per_block + u
            send[rank] = blocks.pack(stage[rank]).astype(BF16)

            @pl.when(rank != me)
            def _():
                to_rank(rank, me).start()

            return 0

        lax.fori_loop(0, per_block, give_one, 0)

    loads[0].wait()
    loads[1].wait()
    first = apply_block(pivots, 0, [forcing[item, span(0)] for item in range(items)])
    for item in range(items):
        solved[item, span(0)] = first[item]
    loads[2].wait()

    def descend(k, carry):
        drop = apply_block(lower, k - 1, carry)
        rest = [forcing[item, span(k)] - drop[item] for item in range(items)]
        now = apply_block(pivots, k, rest)
        for item in range(items):
            solved[item, span(k)] = now[item]
        return tuple(now)

    last = tuple(first)
    if count == 2:
        last = descend(1, last)
    else:
        last = lax.fori_loop(1, count, descend, last)
    loads[3].wait()
    pl.semaphore_wait(barrier, ranks)
    emit(count - 1, last)

    def up_step(step, carry):
        k = count - 2 - step
        drop = apply_block(upper, k, carry)
        now = [solved[item, span(k)] - drop[item] for item in range(items)]
        for item in range(items):
            solved[item, span(k)] = now[item]
        emit(k, now)
        return tuple(now)

    if count == 2:
        up_step(0, last)
    else:
        lax.fori_loop(0, count - 1, up_step, last)
    keep = pltpu.make_async_copy(solved, solved_hbm, solved_sem)
    keep.start()
    message[lat, me] = send[me]
    to_pair(me, lat).start()

    loads[4].wait()
    row = lax.broadcasted_iota(jnp.int32, (8, phi_count), 0)
    column = lax.broadcasted_iota(jnp.int32, (8, phi_count), 1).astype(F32)
    wave = jnp.zeros((8, phi_count), F32)
    for i in range(modes):
        wave = jnp.where(row == i, modes_ref[i].astype(F32), wave)
    turns = wave * column
    turns = turns - phi_count * jnp.floor((turns + 0.5) * (1.0 / phi_count))
    angle = turns * (2.0 * math.pi / phi_count)
    sine, cosine = jnp.sin(angle), jnp.cos(angle)
    factor = wave * (2.0 / degrees)
    slope = [(-factor * t).astype(BF16).astype(F32) for t in (sine, cosine)]
    turn = [(t * (2.0 / phi_count)).astype(BF16).astype(F32) for t in (cosine, -sine)]
    rows = []
    for c in range(2):
        for e in range(2):
            for i in range(modes):
                rows.append(slope[c if e == 0 else 1 - c][i : i + 1] * turn[c])
    table = jnp.concatenate(rows, 0)
    high = table.astype(BF16)
    rest = (table - high.astype(F32)).astype(BF16)
    tables = jnp.concatenate([high, rest], 0)
    across = (((1,), (1,)), ((), ()))
    pairs = 2 * modes * 8
    for r in range(levels):
        value = lax.dot_general(tables, zonal[r], across, preferred_element_type=F32)
        value = value[: 2 * pairs] + value[2 * pairs :]
        for c in range(2):
            for part in range(cycles // LANES):
                waves[part, pl.ds(c * levels + r, pairs, stride=8), :] = value[
                    c * pairs : (c + 1) * pairs, part * LANES : (part + 1) * LANES
                ]

    def lay(at, value):
        here = pl.ds(pl.multiple_of(at, LANES), LANES)
        high = lax.shift_right_arithmetic(slots[:, here], SHIFT)
        for h in range(0, high_count, 2):
            pair = [jnp.where(high == h + n, value, 0.0) for n in range(2)]
            spread[h * values : (h + 2) * values, here] = jnp.concatenate(pair, 0).astype(BF16)

    def lay_main(half, source):
        if blocks.full:
            lay(half * blocks.half + source * LANES, message[half, source].astype(F32)[:values])

    def lay_tails(half):
        share, slot = blocks.share, blocks.slot

        def step(group, _):
            sets = [
                message[half, group * share + d].astype(F32)[base : base + 8]
                for d in range(share)
            ]
            pieces = [
                jnp.concatenate([s[:, g * slot : (g + 1) * slot] for s in sets], 1)
                for g in range(blocks.groups)
            ]
            at = half * blocks.half + blocks.main + group * LANES
            lay(at, jnp.concatenate(pieces, 0))
            return 0

        lax.fori_loop(0, ranks // share, step, 0)

    def hand_on(d, _):
        source = lax.rem(me + ranks - d, ranks)
        to_rank(source, source).wait_recv()
        to_pair(source, lat).start()
        return 0

    lax.fori_loop(1, ranks, hand_on, 0)

    def heat(n, _):
        here = pl.ds(pl.multiple_of(n * LANES, LANES), LANES)
        low = slots[:, here] & (LOW - 1)
        rows = lax.broadcasted_iota(jnp.int32, (LOW, LANES), 0)
        hot[:, here] = jnp.where(rows == low, 1.0, 0.0).astype(BF16)
        return 0

    lax.fori_loop(0, halves * blocks.half // LANES, heat, 0)

    def mine(source, _):
        lay_main(lat, source)
        return 0

    lax.fori_loop(0, ranks, mine, 0)
    lay_tails(lat)

    def theirs(source, _):
        to_pair(source, 1 - lat).wait_recv()
        lay_main(1 - lat, source)
        return 0

    lax.fori_loop(0, ranks, theirs, 0)
    lay_tails(1 - lat)

    coeffs = lax.dot_general(spread[...], hot[...], across, preferred_element_type=F32)
    lane = lax.broadcasted_iota(jnp.int32, (values, LOW), 1)

    def allowed(i, n):
        return lane + n * LOW >= modes_ref[i]

    loads[5].wait()
    for i in range(modes):
        rows = []
        for n in range(chunks):
            at = (i * chunks + n) * values
            rows.append(jnp.where(allowed(i, n), coeffs[at : at + values], 0.0).astype(BF16))
        value = jnp.dot(jnp.concatenate(rows, 1), legendre[i], preferred_element_type=F32)
        value = value.astype(BF16).astype(F32)
        spectral[i] = value
        for f in range(fields):
            turned[i, f * 8 : f * 8 + 8] = pltpu.roll(value[f * 8 : f * 8 + 8], 4, 0)

    sums = []
    for j in range(modes):
        stack = []
        for f in range(fields):
            parts = []
            for part in range(cycles // LANES):
                acc = None
                for e, source in enumerate((spectral, turned)):
                    for i in range(modes):
                        at = ((e * modes + i) * 8 + j) * 8
                        term = (
                            source[i, f * 8 : f * 8 + 8, part * LANES : (part + 1) * LANES]
                            * waves[part, at : at + 8, :]
                        )
                        acc = term if acc is None else acc + term
                parts.append(acc)
            stack.append(jnp.concatenate(parts, 1))
        sums.append((jnp.concatenate(stack, 0) * weight[...]).astype(BF16))

    pieces = []
    for i in range(modes):
        value = lax.dot_general(sums[i], legendre[i], across, preferred_element_type=F32)
        for n in range(chunks):
            piece = value[:, n * LOW : (n + 1) * LOW]
            pieces.append(jnp.where(allowed(i, n), piece, 0.0))
    advection = jnp.concatenate(pieces, 0).astype(BF16)

    wide = 2 * LANES

    def collect(at):
        here = pl.ds(pl.multiple_of(at, LANES), wide)
        value = jnp.dot(advection, hot[:, here], preferred_element_type=F32)
        high = lax.shift_right_arithmetic(slots[:, here], SHIFT)
        acc = jnp.zeros((values, wide), F32)
        for h in range(high_count):
            acc = jnp.where(high == h, value[h * values : (h + 1) * values], acc)
        return acc

    def collect_half(half, handle):
        slot = blocks.slot
        many = wide // slot

        def tail_step(n, _):
            value = collect(half * blocks.half + blocks.main + n * wide)
            for d in range(many):
                tails[n * many + d] = blocks.lanes(
                    [
                        value[g * 8 : g * 8 + 8, d * slot : (d + 1) * slot]
                        for g in range(blocks.groups)
                    ]
                )
            return 0

        lax.fori_loop(0, ranks // many, tail_step, 0)

        if blocks.full:

            def main_step(n, _):
                turn = lax.rem(me // 2 + 1 + n, ranks // 2)
                value = collect(half * blocks.half + turn * wide)
                for u in range(2):
                    rank = turn * 2 + u
                    handle(
                        rank, blocks.join(value[:, u * LANES : (u + 1) * LANES], tails[rank])
                    )
                return 0

            lax.fori_loop(0, ranks // 2, main_step, 0)
        else:

            def rank_step(n, _):
                rank = lax.rem(me + 1 + n, ranks)
                handle(rank, blocks.join(None, tails[rank]))
                return 0

            lax.fori_loop(0, ranks, rank_step, 0)

    def pair_back(rank):
        return pltpu.make_async_remote_copy(
            src_ref=give.at[rank], dst_ref=other.at[rank],
            send_sem=pass2_sem.at[rank], recv_sem=got2_sem.at[rank],
            device_id=(me, 1 - lat), device_id_type=MESH,
        )

    def rank_back(rank, source):
        return pltpu.make_async_remote_copy(
            src_ref=total.at[rank], dst_ref=back.at[source],
            send_sem=send2_sem.at[rank], recv_sem=recv2_sem.at[source],
            device_id=(rank, lat), device_id_type=MESH,
        )

    def to_other(rank, block):
        give[rank] = block.astype(BF16)
        pair_back(rank).start()

    def to_owner(rank, block):
        pair_back(rank).wait_recv()
        total[rank] = (block + other[rank].astype(F32)).astype(BF16)

        @pl.when(rank != me)
        def _():
            rank_back(rank, me).start()

    collect_half(1 - lat, to_other)
    collect_half(lat, to_owner)
    back[me] = total[me]

    def sent(d, _):
        rank = lax.rem(me + d, ranks)
        to_rank(rank, me).wait_send()
        to_pair(rank, lat).wait_send()
        pair_back(rank).wait_send()
        return 0

    lax.fori_loop(1, ranks, sent, 0)
    to_pair(me, lat).wait_send()
    pair_back(me).wait_send()
    keep.wait()

    def arrived(d, _):
        source = lax.rem(me + ranks - d, ranks)
        rank_back(source, source).wait_recv()
        return 0

    lax.fori_loop(1, ranks, arrived, 0)

    edge = 8
    held[:, 0:edge, :] = jnp.zeros((items, edge, columns), F32)
    held[:, edge + depth : 2 * edge + depth, :] = jnp.zeros((items, edge, columns), F32)
    for rank in range(ranks):
        value = back[rank].astype(F32)
        tail = jnp.concatenate(
            [
                value[base : base + 8, g * blocks.slot : g * blocks.slot + blocks.tail]
                for g in range(blocks.groups)
            ],
            0,
        )
        at = edge + rank * levels
        for item in range(items):
            here = slice(item * levels, (item + 1) * levels)
            if blocks.full:
                held[item, at : at + levels, 0:LANES] = value[here]
            held[item, at : at + levels, blocks.full * LANES : columns] = tail[here]

    scale = spacing[...]
    for item in range(items):

        def shifted(n):
            return held[item, edge + n : edge + n + depth, :]

        slant = shifted(-2) - 8.0 * shifted(-1) + 8.0 * shifted(1) - shifted(2)
        out[item] = shifted(0) + scale * slant

    def sent_back(d, _):
        rank_back(lax.rem(me + d, ranks), me).wait_send()
        return 0

    lax.fori_loop(1, ranks, sent_back, 0)


def body(
    forcing,
    pivots,
    lower,
    upper,
    slab_modes,
    slot_of_column,
    legendre,
    cycle_weight,
    zonal_flow,
    inverse_spacing,
):
    ranks, halves = lax.axis_size("rad"), lax.axis_size("lat")
    columns, depth = forcing.shape[2], forcing.shape[3]
    modes, degrees, cycles = legendre.shape
    levels = zonal_flow.shape[0]
    items = 6
    values = items * levels
    blocks = Blocks(columns, values, ranks)
    line = (ranks, blocks.rows, LANES)
    total = halves * blocks.half
    matrices = [m.transpose(1, 2, 3, 0) for m in (pivots, lower, upper)]
    right = forcing.transpose(0, 1, 3, 2).reshape(items, depth, columns)
    sizes = [right, *matrices, zonal_flow, legendre]

    solved, explicit = pl.pallas_call(
        functools.partial(kernel, blocks, halves),
        out_shape=(jax.ShapeDtypeStruct((items, depth, columns), F32),) * 2,
        in_specs=[SMEM] + [VMEM] * 3 + [ANY] * 6,
        out_specs=(ANY, VMEM),
        scratch_shapes=[pltpu.VMEM(x.shape, x.dtype) for x in sizes]
        + [
            pltpu.VMEM((items, depth, columns), F32),
            pltpu.VMEM((ranks, values, columns), F32),
            pltpu.VMEM(line, BF16),
            pltpu.VMEM((halves,) + line, BF16),
            pltpu.VMEM((LOW, total), BF16),
            pltpu.VMEM((modes * (degrees // LOW) * values, total), BF16),
            pltpu.VMEM((cycles // LANES, 2 * modes * 8 * 8, LANES), F32),
            pltpu.VMEM((modes, values, cycles), F32),
            pltpu.VMEM((modes, values, cycles), F32),
            pltpu.VMEM((ranks, 8, LANES), F32),
            pltpu.VMEM(line, BF16),
            pltpu.VMEM(line, BF16),
            pltpu.VMEM(line, BF16),
            pltpu.VMEM(line, BF16),
            pltpu.VMEM((items, depth + 16, columns), F32),
            pltpu.SemaphoreType.DMA((6,)),
            pltpu.SemaphoreType.DMA,
        ]
        + [pltpu.SemaphoreType.DMA((ranks,))] * 8,
        compiler_params=pltpu.CompilerParams(
            vmem_limit_bytes=ROOM, collective_id=0, has_side_effects=True
        ),
        name="step",
    )(
        slab_modes, blocks.order(slot_of_column, halves), inverse_spacing[:, None],
        cycle_weight[None], right, *matrices, zonal_flow, legendre,
    )

    def placed(value):
        return value.reshape(3, 2, depth, columns).transpose(0, 1, 3, 2)

    return (placed(solved), placed(explicit))


def solution(mesh):
    placed = (
        P(None, None, ("rad", "lat"), None),
        P(("rad", "lat"), None, None, None),
        P(("rad", "lat"), None, None, None),
        P(("rad", "lat"), None, None, None),
        P(),
        P(),
        P(None, None, "lat"),
        P("lat"),
        P("rad", "lat", None),
        P(),
    )
    return jax.shard_map(
        body,
        mesh=mesh,
        in_specs=placed,
        out_specs=(P(None, None, ("rad", "lat"), None), P(None, None, ("rad", "lat"), None)),
        check_vma=False,
    )
```

```python
import functools
import math

import jax
import jax.numpy as jnp
from jax import lax
from jax.experimental import pallas as pl
from jax.experimental.pallas import tpu as pltpu
from jax.sharding import PartitionSpec as P

LANES = 128
SHIFT = 8
LOW = 1 << SHIFT
MESH = pl.DeviceIdType.MESH
VMEM = pl.BlockSpec(memory_space=pltpu.VMEM)
SMEM = pl.BlockSpec(memory_space=pltpu.SMEM)
ANY = pl.BlockSpec(memory_space=pl.ANY)
F32 = jnp.float32
BF16 = jnp.bfloat16
ROOM = 60 * 1024 * 1024


class Blocks:
    def __init__(self, columns, values, ranks):
        self.columns, self.values, self.ranks = columns, values, ranks
        self.full, self.tail = divmod(columns, LANES)
        self.groups = values // 8
        self.slot = 8
        while self.slot < self.tail:
            self.slot *= 2
        assert self.full <= 1 and self.slot * self.groups <= LANES
        self.base = self.full * values
        self.rows = -(-(self.base + 8) // 16) * 16
        self.share = LANES // self.slot
        self.main = ranks * self.full * LANES
        self.half = self.main + ranks * self.slot

    def join(self, main, tail):
        parts = ([main] if self.full else []) + [tail]
        spare = self.rows - self.base - 8
        if spare:
            parts.append(jnp.zeros((spare, LANES), tail.dtype))
        return jnp.concatenate(parts, 0)

    def lanes(self, pieces):
        parts = []
        for piece in pieces:
            parts.append(piece)
            if piece.shape[1] < self.slot:
                parts.append(jnp.zeros((8, self.slot - piece.shape[1]), piece.dtype))
        spare = LANES - self.slot * len(pieces)
        if spare:
            parts.append(jnp.zeros((8, spare), pieces[0].dtype))
        return jnp.concatenate(parts, 1)

    def pack(self, value):
        rest = value[:, self.full * LANES :]
        tail = self.lanes([rest[8 * g : 8 * g + 8] for g in range(self.groups)])
        return self.join(value[:, : self.full * LANES], tail)

    def order(self, raw, halves, slots):
        table = raw[...][None, :]
        for half in range(halves):
            for rank in range(self.ranks):
                at = (rank * halves + half) * self.columns
                if self.full:
                    here = half * self.half + rank * LANES
                    slots[:, here : here + LANES] = table[:, at : at + LANES]
                    at += LANES
            for first in range(0, self.ranks, self.share):
                parts = []
                for rank in range(first, first + self.share):
                    at = (rank * halves + half) * self.columns + self.full * LANES
                    parts.append(table[:, at : at + self.tail])
                    if self.slot > self.tail:
                        parts.append(jnp.full((1, self.slot - self.tail), -1, jnp.int32))
                here = half * self.half + self.main + first * self.slot
                slots[:, here : here + LANES] = jnp.concatenate(parts, 1)


def sublane_sums(values):
    row = lax.broadcasted_iota(jnp.int32, values[0].shape, 0)
    step = 1
    while len(values) > 1:
        keep = (row & step) == 0
        merged = []
        for first, second in zip(values[0::2], values[1::2]):
            straight = jnp.where(keep, first, second)
            crossed = jnp.where(keep, second, first)
            merged.append(straight + pltpu.roll(crossed, step, 0))
        values, step = merged, step * 2
    return values[0]


def kernel(
    blocks, halves, modes_ref, raw_slots, weight, forcing_hbm, pivots_hbm, lower_hbm,
    upper_hbm, zonal_hbm, legendre_hbm, solved_hbm, back,
    slots, forcing, pivots, lower, upper, zonal, legendre, solved, stage, send, message, hot, spread,
    waves, spectral, turned, tails, give, other, total,
    load_sem, solved_sem, send_sem, recv_sem, pass_sem, got_sem,
    send2_sem, recv2_sem, pass2_sem, got2_sem,
):
    me, lat = lax.axis_index("rad"), lax.axis_index("lat")
    ranks, values, base = blocks.ranks, blocks.values, blocks.base
    items, depth, columns = forcing.shape
    count, size = pivots.shape[0], pivots.shape[1]
    levels = depth // ranks
    modes, degrees, cycles = legendre.shape
    phi_count = zonal.shape[2]
    chunks = degrees // LOW
    high_count = modes * chunks
    fields = values // 8

    loads = [
        pltpu.make_async_copy(source, target, load_sem.at[n])
        for n, (source, target) in enumerate(
            (
                (forcing_hbm, forcing), (pivots_hbm, pivots), (lower_hbm, lower),
                (upper_hbm, upper), (zonal_hbm, zonal), (legendre_hbm, legendre),
            )
        )
    ]
    for load in loads[:4]:
        load.start()

    barrier = pltpu.get_barrier_semaphore()
    pl.semaphore_signal(barrier, inc=1, device_id=(me, 1 - lat), device_id_type=MESH)

    def hello(d, _):
        rank = lax.rem(me + d, ranks)
        pl.semaphore_signal(barrier, inc=1, device_id=(rank, lat), device_id_type=MESH)
        return 0

    lax.fori_loop(1, ranks, hello, 0)

    def to_rank(rank, source):
        return pltpu.make_async_remote_copy(
            src_ref=send.at[rank], dst_ref=message.at[lat, source],
            send_sem=send_sem.at[rank], recv_sem=recv_sem.at[source],
            device_id=(rank, lat), device_id_type=MESH,
        )

    def to_pair(source, half):
        return pltpu.make_async_remote_copy(
            src_ref=message.at[lat, source], dst_ref=message.at[half, source],
            send_sem=pass_sem.at[source], recv_sem=got_sem.at[source],
            device_id=(me, 1 - lat), device_id_type=MESH,
        )

    def apply_block(matrix, at, vectors):
        pieces = [[] for _ in vectors]
        for i in range(0, size, 8):
            for item, vector in enumerate(vectors):
                sums = []
                for n in range(8):
                    acc = matrix[at, i + n, 0:8] * vector[0:8]
                    for j in range(8, size, 8):
                        acc = acc + matrix[at, i + n, j : j + 8] * vector[j : j + 8]
                    sums.append(acc)
                pieces[item].append(sublane_sums(sums))
        return [jnp.concatenate(p, 0) for p in pieces]

    def span(k):
        return pl.ds(k * size if isinstance(k, int) else pl.multiple_of(k * size, size), size)

    per_block = size // levels

    def emit(k, vectors):
        for u in range(per_block):
            for item in range(items):
                stage[k * per_block + u, item * levels : (item + 1) * levels, :] = vectors[item][
                    u * levels : (u + 1) * levels
                ]

        def give_one(u, _):
            rank = k * per_block + u
            send[rank] = blocks.pack(stage[rank]).astype(BF16)

            @pl.when(rank != me)
            def _():
                to_rank(rank, me).start()

            return 0

        lax.fori_loop(0, per_block, give_one, 0)

    loads[0].wait()
    loads[1].wait()
    first = apply_block(pivots, 0, [forcing[item, span(0)] for item in range(items)])
    for item in range(items):
        solved[item, span(0)] = first[item]
    loads[2].wait()
    loads[4].start()

    def descend(k, carry):
        drop = apply_block(lower, k - 1, carry)
        rest = [forcing[item, span(k)] - drop[item] for item in range(items)]
        now = apply_block(pivots, k, rest)
        for item in range(items):
            solved[item, span(k)] = now[item]
        return tuple(now)

    last = tuple(first)
    if count == 2:
        last = descend(1, last)
    else:
        last = lax.fori_loop(1, count, descend, last)
    loads[3].wait()
    pl.semaphore_wait(barrier, ranks)
    emit(count - 1, last)

    def up_step(step, carry):
        k = count - 2 - step
        drop = apply_block(upper, k, carry)
        now = [solved[item, span(k)] - drop[item] for item in range(items)]
        for item in range(items):
            solved[item, span(k)] = now[item]
        emit(k, now)
        return tuple(now)

    if count == 2:
        up_step(0, last)
    else:
        lax.fori_loop(0, count - 1, up_step, last)
    keep = pltpu.make_async_copy(solved, solved_hbm, solved_sem)
    keep.start()
    message[lat, me] = send[me]
    to_pair(me, lat).start()

    loads[4].wait()
    loads[5].start()
    row = lax.broadcasted_iota(jnp.int32, (8, phi_count), 0)
    column = lax.broadcasted_iota(jnp.int32, (8, phi_count), 1).astype(F32)
    wave = jnp.zeros((8, phi_count), F32)
    for i in range(modes):
        wave = jnp.where(row == i, modes_ref[i].astype(F32), wave)
    turns = wave * column
    turns = turns - phi_count * jnp.floor((turns + 0.5) * (1.0 / phi_count))
    angle = turns * (2.0 * math.pi / phi_count)
    sine, cosine = jnp.sin(angle), jnp.cos(angle)
    factor = wave * (2.0 / degrees)
    slope = [(-factor * t).astype(BF16).astype(F32) for t in (sine, cosine)]
    turn = [(t * (2.0 / phi_count)).astype(BF16).astype(F32) for t in (cosine, -sine)]
    rows = []
    for c in range(2):
        for e in range(2):
            for i in range(modes):
                rows.append(slope[c if e == 0 else 1 - c][i : i + 1] * turn[c])
    table = jnp.concatenate(rows, 0)
    high = table.astype(BF16)
    rest = (table - high.astype(F32)).astype(BF16)
    tables = jnp.concatenate([high, rest], 0)
    across = (((1,), (1,)), ((), ()))
    pairs = 2 * modes * 8
    for r in range(levels):
        value = lax.dot_general(tables, zonal[r], across, preferred_element_type=F32)
        value = value[: 2 * pairs] + value[2 * pairs :]
        for c in range(2):
            for part in range(cycles // LANES):
                waves[part, pl.ds(c * levels + r, pairs, stride=8), :] = value[
                    c * pairs : (c + 1) * pairs, part * LANES : (part + 1) * LANES
                ]

    def lay(at, value):
        here = pl.ds(pl.multiple_of(at, LANES), LANES)
        high = lax.shift_right_arithmetic(slots[:, here], SHIFT)
        for h in range(0, high_count, 2):
            pair = [jnp.where(high == h + n, value, 0.0) for n in range(2)]
            spread[h * values : (h + 2) * values, here] = jnp.concatenate(pair, 0).astype(BF16)

    def lay_main(half, source):
        if blocks.full:
            lay(half * blocks.half + source * LANES, message[half, source].astype(F32)[:values])

    def lay_tails(half):
        share, slot = blocks.share, blocks.slot

        def step(group, _):
            sets = [
                message[half, group * share + d].astype(F32)[base : base + 8]
                for d in range(share)
            ]
            pieces = [
                jnp.concatenate([s[:, g * slot : (g + 1) * slot] for s in sets], 1)
                for g in range(blocks.groups)
            ]
            at = half * blocks.half + blocks.main + group * LANES
            lay(at, jnp.concatenate(pieces, 0))
            return 0

        lax.fori_loop(0, ranks // share, step, 0)

    def hand_on(d, _):
        source = lax.rem(me + ranks - d, ranks)
        to_rank(source, source).wait_recv()
        to_pair(source, lat).start()
        return 0

    lax.fori_loop(1, ranks, hand_on, 0)

    blocks.order(raw_slots, halves, slots)

    def heat(n, _):
        here = pl.ds(pl.multiple_of(n * LANES, LANES), LANES)
        low = slots[:, here] & (LOW - 1)
        rows = lax.broadcasted_iota(jnp.int32, (LOW, LANES), 0)
        hot[:, here] = jnp.where(rows == low, 1.0, 0.0).astype(BF16)
        return 0

    lax.fori_loop(0, halves * blocks.half // LANES, heat, 0)

    def mine(source, _):
        lay_main(lat, source)
        return 0

    lax.fori_loop(0, ranks, mine, 0)
    lay_tails(lat)

    def theirs(source, _):
        to_pair(source, 1 - lat).wait_recv()
        lay_main(1 - lat, source)
        return 0

    lax.fori_loop(0, ranks, theirs, 0)
    lay_tails(1 - lat)

    coeffs = lax.dot_general(spread[...], hot[...], across, preferred_element_type=F32)
    lane = lax.broadcasted_iota(jnp.int32, (values, LOW), 1)

    def allowed(i, n):
        return lane + n * LOW >= modes_ref[i]

    loads[5].wait()
    for i in range(modes):
        rows = []
        for n in range(chunks):
            at = (i * chunks + n) * values
            rows.append(jnp.where(allowed(i, n), coeffs[at : at + values], 0.0).astype(BF16))
        value = jnp.dot(jnp.concatenate(rows, 1), legendre[i], preferred_element_type=F32)
        value = value.astype(BF16).astype(F32)
        spectral[i] = value
        for f in range(fields):
            turned[i, f * 8 : f * 8 + 8] = pltpu.roll(value[f * 8 : f * 8 + 8], 4, 0)

    sums = []
    for j in range(modes):
        stack = []
        for f in range(fields):
            parts = []
            for part in range(cycles // LANES):
                acc = None
                for e, source in enumerate((spectral, turned)):
                    for i in range(modes):
                        at = ((e * modes + i) * 8 + j) * 8
                        term = (
                            source[i, f * 8 : f * 8 + 8, part * LANES : (part + 1) * LANES]
                            * waves[part, at : at + 8, :]
                        )
                        acc = term if acc is None else acc + term
                parts.append(acc)
            stack.append(jnp.concatenate(parts, 1))
        sums.append((jnp.concatenate(stack, 0) * weight[...][None, :]).astype(BF16))

    pieces = []
    for i in range(modes):
        value = lax.dot_general(sums[i], legendre[i], across, preferred_element_type=F32)
        for n in range(chunks):
            piece = value[:, n * LOW : (n + 1) * LOW]
            pieces.append(jnp.where(allowed(i, n), piece, 0.0))
    advection = jnp.concatenate(pieces, 0).astype(BF16)

    wide = 2 * LANES

    def collect(at):
        here = pl.ds(pl.multiple_of(at, LANES), wide)
        value = jnp.dot(advection, hot[:, here], preferred_element_type=F32)
        high = lax.shift_right_arithmetic(slots[:, here], SHIFT)
        acc = jnp.zeros((values, wide), F32)
        for h in range(high_count):
            acc = jnp.where(high == h, value[h * values : (h + 1) * values], acc)
        return acc

    def collect_half(half, handle):
        slot = blocks.slot
        many = wide // slot

        def tail_step(n, _):
            value = collect(half * blocks.half + blocks.main + n * wide)
            for d in range(many):
                tails[n * many + d] = blocks.lanes(
                    [
                        value[g * 8 : g * 8 + 8, d * slot : (d + 1) * slot]
                        for g in range(blocks.groups)
                    ]
                )
            return 0

        lax.fori_loop(0, ranks // many, tail_step, 0)

        if blocks.full:

            def main_step(n, _):
                turn = lax.rem(me // 2 + 1 + n, ranks // 2)
                value = collect(half * blocks.half + turn * wide)
                for u in range(2):
                    rank = turn * 2 + u
                    handle(
                        rank, blocks.join(value[:, u * LANES : (u + 1) * LANES], tails[rank])
                    )
                return 0

            lax.fori_loop(0, ranks // 2, main_step, 0)
        else:

            def rank_step(n, _):
                rank = lax.rem(me + 1 + n, ranks)
                handle(rank, blocks.join(None, tails[rank]))
                return 0

            lax.fori_loop(0, ranks, rank_step, 0)

    def pair_back(rank):
        return pltpu.make_async_remote_copy(
            src_ref=give.at[rank], dst_ref=other.at[rank],
            send_sem=pass2_sem.at[rank], recv_sem=got2_sem.at[rank],
            device_id=(me, 1 - lat), device_id_type=MESH,
        )

    def rank_back(rank, source):
        return pltpu.make_async_remote_copy(
            src_ref=total.at[rank], dst_ref=back.at[source],
            send_sem=send2_sem.at[rank], recv_sem=recv2_sem.at[source],
            device_id=(rank, lat), device_id_type=MESH,
        )

    def to_other(rank, block):
        give[rank] = block.astype(BF16)
        pair_back(rank).start()

    def to_owner(rank, block):
        pair_back(rank).wait_recv()
        total[rank] = (block + other[rank].astype(F32)).astype(BF16)

        @pl.when(rank != me)
        def _():
            rank_back(rank, me).start()

    collect_half(1 - lat, to_other)
    collect_half(lat, to_owner)
    back[me] = total[me]

    def sent(d, _):
        rank = lax.rem(me + d, ranks)
        to_rank(rank, me).wait_send()
        to_pair(rank, lat).wait_send()
        pair_back(rank).wait_send()
        return 0

    lax.fori_loop(1, ranks, sent, 0)
    to_pair(me, lat).wait_send()
    pair_back(me).wait_send()
    keep.wait()

    def arrived(d, _):
        source = lax.rem(me + ranks - d, ranks)
        rank_back(source, source).wait_recv()
        return 0

    lax.fori_loop(1, ranks, arrived, 0)

    def sent_back(d, _):
        rank_back(lax.rem(me + d, ranks), me).wait_send()
        return 0

    lax.fori_loop(1, ranks, sent_back, 0)


def last_kernel(blocks, spacing, back, solved, solved_out, out, held, solved_sem):
    ranks, values, base = blocks.ranks, blocks.values, blocks.base
    items, depth, columns = out.shape
    levels = depth // ranks
    hand_on = pltpu.make_async_copy(solved, solved_out, solved_sem)
    hand_on.start()
    edge = 8
    held[:, 0:edge, :] = jnp.zeros((items, edge, columns), F32)
    held[:, edge + depth : 2 * edge + depth, :] = jnp.zeros((items, edge, columns), F32)
    for rank in range(ranks):
        value = back[rank].astype(F32)
        tail = jnp.concatenate(
            [
                value[base : base + 8, g * blocks.slot : g * blocks.slot + blocks.tail]
                for g in range(blocks.groups)
            ],
            0,
        )
        at = edge + rank * levels
        for item in range(items):
            here = slice(item * levels, (item + 1) * levels)
            if blocks.full:
                held[item, at : at + levels, 0:LANES] = value[here]
            held[item, at : at + levels, blocks.full * LANES : columns] = tail[here]

    keep = lax.broadcasted_iota(jnp.int32, (depth, depth), 0) == lax.broadcasted_iota(
        jnp.int32, (depth, depth), 1
    )
    scale = jnp.sum(jnp.where(keep, spacing[...][None, :], 0.0), axis=1, keepdims=True)
    for item in range(items):

        def shifted(n):
            return held[item, edge + n : edge + n + depth, :]

        slant = shifted(-2) - 8.0 * shifted(-1) + 8.0 * shifted(1) - shifted(2)
        out[item] = shifted(0) + scale * slant

    hand_on.wait()


def body(
    forcing,
    pivots,
    lower,
    upper,
    slab_modes,
    slot_of_column,
    legendre,
    cycle_weight,
    zonal_flow,
    inverse_spacing,
):
    ranks, halves = lax.axis_size("rad"), lax.axis_size("lat")
    columns, depth = forcing.shape[2], forcing.shape[3]
    modes, degrees, cycles = legendre.shape
    levels = zonal_flow.shape[0]
    items = 6
    values = items * levels
    blocks = Blocks(columns, values, ranks)
    line = (ranks, blocks.rows, LANES)
    total = halves * blocks.half
    matrices = [m.transpose(1, 2, 3, 0) for m in (pivots, lower, upper)]
    right = forcing.transpose(0, 1, 3, 2).reshape(items, depth, columns)
    sizes = [right, *matrices, zonal_flow, legendre]

    grid = jax.ShapeDtypeStruct((items, depth, columns), F32)

    solved, back = pl.pallas_call(
        functools.partial(kernel, blocks, halves),
        out_shape=(grid, jax.ShapeDtypeStruct(line, BF16)),
        in_specs=[SMEM] + [VMEM] * 2 + [ANY] * 6,
        out_specs=(ANY, VMEM),
        scratch_shapes=[pltpu.VMEM((1, total), jnp.int32)]
        + [pltpu.VMEM(x.shape, x.dtype) for x in sizes]
        + [
            pltpu.VMEM((items, depth, columns), F32),
            pltpu.VMEM((ranks, values, columns), F32),
            pltpu.VMEM(line, BF16),
            pltpu.VMEM((halves,) + line, BF16),
            pltpu.VMEM((LOW, total), BF16),
            pltpu.VMEM((modes * (degrees // LOW) * values, total), BF16),
            pltpu.VMEM((cycles // LANES, 2 * modes * 8 * 8, LANES), F32),
            pltpu.VMEM((modes, values, cycles), F32),
            pltpu.VMEM((modes, values, cycles), F32),
            pltpu.VMEM((ranks, 8, LANES), F32),
            pltpu.VMEM(line, BF16),
            pltpu.VMEM(line, BF16),
            pltpu.VMEM(line, BF16),
            pltpu.SemaphoreType.DMA((6,)),
            pltpu.SemaphoreType.DMA,
        ]
        + [pltpu.SemaphoreType.DMA((ranks,))] * 8,
        compiler_params=pltpu.CompilerParams(
            vmem_limit_bytes=ROOM, collective_id=0, has_side_effects=True
        ),
        name="step",
    )(slab_modes, slot_of_column, cycle_weight, right, *matrices, zonal_flow, legendre)

    solved, explicit = pl.pallas_call(
        functools.partial(last_kernel, blocks),
        out_shape=(grid, grid),
        in_specs=[VMEM, VMEM, ANY],
        out_specs=(ANY, VMEM),
        scratch_shapes=[
            pltpu.VMEM((items, depth + 16, columns), F32),
            pltpu.SemaphoreType.DMA,
        ],
        compiler_params=pltpu.CompilerParams(vmem_limit_bytes=ROOM),
        name="stencil",
    )(inverse_spacing, back, solved)

    def placed(value):
        return value.reshape(3, 2, depth, columns).transpose(0, 1, 3, 2)

    return (placed(solved), placed(explicit))


def solution(mesh):
    placed = (
        P(None, None, ("rad", "lat"), None),
        P(("rad", "lat"), None, None, None),
        P(("rad", "lat"), None, None, None),
        P(("rad", "lat"), None, None, None),
        P(),
        P(),
        P(None, None, "lat"),
        P("lat"),
        P("rad", "lat", None),
        P(),
    )
    return jax.shard_map(
        body,
        mesh=mesh,
        in_specs=placed,
        out_specs=(P(None, None, ("rad", "lat"), None), P(None, None, ("rad", "lat"), None)),
        check_vma=False,
    )
```

```python
import functools
import math

import jax
import jax.numpy as jnp
from jax import lax
from jax.experimental import pallas as pl
from jax.experimental.pallas import tpu as pltpu
from jax.sharding import PartitionSpec as P

LANES = 128
SHIFT = 8
LOW = 1 << SHIFT
MESH = pl.DeviceIdType.MESH
VMEM = pl.BlockSpec(memory_space=pltpu.VMEM)
SMEM = pl.BlockSpec(memory_space=pltpu.SMEM)
ANY = pl.BlockSpec(memory_space=pl.ANY)
F32 = jnp.float32
BF16 = jnp.bfloat16
ROOM = 60 * 1024 * 1024


class Blocks:
    def __init__(self, columns, values, ranks):
        self.columns, self.values, self.ranks = columns, values, ranks
        self.full, self.tail = divmod(columns, LANES)
        self.groups = values // 8
        self.slot = 8
        while self.slot < self.tail:
            self.slot *= 2
        assert self.full <= 1 and self.slot * self.groups <= LANES
        self.base = self.full * values
        self.rows = -(-(self.base + 8) // 16) * 16
        self.share = LANES // self.slot
        self.main = ranks * self.full * LANES
        self.half = self.main + ranks * self.slot

    def join(self, main, tail):
        parts = ([main] if self.full else []) + [tail]
        spare = self.rows - self.base - 8
        if spare:
            parts.append(jnp.zeros((spare, LANES), tail.dtype))
        return jnp.concatenate(parts, 0)

    def lanes(self, pieces):
        parts = []
        for piece in pieces:
            parts.append(piece)
            if piece.shape[1] < self.slot:
                parts.append(jnp.zeros((8, self.slot - piece.shape[1]), piece.dtype))
        spare = LANES - self.slot * len(pieces)
        if spare:
            parts.append(jnp.zeros((8, spare), pieces[0].dtype))
        return jnp.concatenate(parts, 1)

    def pack(self, value):
        rest = value[:, self.full * LANES :]
        tail = self.lanes([rest[8 * g : 8 * g + 8] for g in range(self.groups)])
        return self.join(value[:, : self.full * LANES], tail)

    def order(self, raw, halves, slots):
        table = raw[...][None, :]
        for half in range(halves):
            for rank in range(self.ranks):
                at = (rank * halves + half) * self.columns
                if self.full:
                    here = half * self.half + rank * LANES
                    slots[:, here : here + LANES] = table[:, at : at + LANES]
                    at += LANES
            for first in range(0, self.ranks, self.share):
                parts = []
                for rank in range(first, first + self.share):
                    at = (rank * halves + half) * self.columns + self.full * LANES
                    parts.append(table[:, at : at + self.tail])
                    if self.slot > self.tail:
                        parts.append(jnp.full((1, self.slot - self.tail), -1, jnp.int32))
                here = half * self.half + self.main + first * self.slot
                slots[:, here : here + LANES] = jnp.concatenate(parts, 1)


def sublane_sums(values):
    row = lax.broadcasted_iota(jnp.int32, values[0].shape, 0)
    step = 1
    while len(values) > 1:
        keep = (row & step) == 0
        merged = []
        for first, second in zip(values[0::2], values[1::2]):
            straight = jnp.where(keep, first, second)
            crossed = jnp.where(keep, second, first)
            merged.append(straight + pltpu.roll(crossed, step, 0))
        values, step = merged, step * 2
    return values[0]


def kernel(
    blocks, halves, modes_ref, raw_slots, weight, forcing_hbm, pivots_hbm, lower_hbm,
    upper_hbm, zonal_hbm, legendre_hbm, solved_hbm, back,
    slots, forcing, pivots, lower, upper, zonal, legendre, solved, stage, send, message, hot, spread,
    waves, spectral, turned, tails, give, other, total,
    load_sem, solved_sem, send_sem, recv_sem, pass_sem, got_sem,
    send2_sem, recv2_sem, pass2_sem, got2_sem,
):
    me, lat = lax.axis_index("rad"), lax.axis_index("lat")
    ranks, values, base = blocks.ranks, blocks.values, blocks.base
    items, depth, columns = forcing.shape
    count, size = pivots.shape[0], pivots.shape[1]
    levels = depth // ranks
    modes, degrees, cycles = legendre.shape
    phi_count = zonal.shape[2]
    chunks = degrees // LOW
    high_count = modes * chunks
    fields = values // 8

    def load(n, source, target):
        return pltpu.make_async_copy(source, target, load_sem.at[n])

    load_right = load(0, forcing_hbm, forcing)
    load_first = load(1, pivots_hbm.at[0], pivots.at[0])
    load_rest = load(2, pivots_hbm.at[pl.ds(1, count - 1)], pivots.at[pl.ds(1, count - 1)])
    load_lower = load(3, lower_hbm, lower)
    load_upper = load(4, upper_hbm, upper)
    load_zonal = load(5, zonal_hbm, zonal)
    load_legendre = load(6, legendre_hbm, legendre)
    for one in (load_right, load_first, load_lower, load_rest, load_upper):
        one.start()

    barrier = pltpu.get_barrier_semaphore()
    pl.semaphore_signal(barrier, inc=1, device_id=(me, 1 - lat), device_id_type=MESH)

    def hello(d, _):
        rank = lax.rem(me + d, ranks)
        pl.semaphore_signal(barrier, inc=1, device_id=(rank, lat), device_id_type=MESH)
        return 0

    lax.fori_loop(1, ranks, hello, 0)

    def to_rank(rank, source):
        return pltpu.make_async_remote_copy(
            src_ref=send.at[rank], dst_ref=message.at[lat, source],
            send_sem=send_sem.at[rank], recv_sem=recv_sem.at[source],
            device_id=(rank, lat), device_id_type=MESH,
        )

    def to_pair(source, half):
        return pltpu.make_async_remote_copy(
            src_ref=message.at[lat, source], dst_ref=message.at[half, source],
            send_sem=pass_sem.at[source], recv_sem=got_sem.at[source],
            device_id=(me, 1 - lat), device_id_type=MESH,
        )

    def apply_block(matrix, at, vectors):
        pieces = [[] for _ in vectors]
        for i in range(0, size, 8):
            for item, vector in enumerate(vectors):
                sums = []
                for n in range(8):
                    acc = matrix[at, i + n, 0:8] * vector[0:8]
                    for j in range(8, size, 8):
                        acc = acc + matrix[at, i + n, j : j + 8] * vector[j : j + 8]
                    sums.append(acc)
                pieces[item].append(sublane_sums(sums))
        return [jnp.concatenate(p, 0) for p in pieces]

    def span(k):
        return pl.ds(k * size if isinstance(k, int) else pl.multiple_of(k * size, size), size)

    per_block = size // levels

    def emit(k, vectors):
        for u in range(per_block):
            for item in range(items):
                stage[k * per_block + u, item * levels : (item + 1) * levels, :] = vectors[item][
                    u * levels : (u + 1) * levels
                ]

        def give_one(u, _):
            rank = k * per_block + u
            send[rank] = blocks.pack(stage[rank]).astype(BF16)

            @pl.when(rank != me)
            def _():
                to_rank(rank, me).start()

            return 0

        lax.fori_loop(0, per_block, give_one, 0)

    load_right.wait()
    load_first.wait()
    first = apply_block(pivots, 0, [forcing[item, span(0)] for item in range(items)])
    for item in range(items):
        solved[item, span(0)] = first[item]
    load_lower.wait()
    load_rest.wait()
    load_zonal.start()

    def descend(k, carry):
        drop = apply_block(lower, k - 1, carry)
        rest = [forcing[item, span(k)] - drop[item] for item in range(items)]
        now = apply_block(pivots, k, rest)
        for item in range(items):
            solved[item, span(k)] = now[item]
        return tuple(now)

    last = tuple(first)
    if count == 2:
        last = descend(1, last)
    else:
        last = lax.fori_loop(1, count, descend, last)
    load_upper.wait()
    pl.semaphore_wait(barrier, ranks)
    emit(count - 1, last)

    def up_step(step, carry):
        k = count - 2 - step
        drop = apply_block(upper, k, carry)
        now = [solved[item, span(k)] - drop[item] for item in range(items)]
        for item in range(items):
            solved[item, span(k)] = now[item]
        emit(k, now)
        return tuple(now)

    if count == 2:
        up_step(0, last)
    else:
        lax.fori_loop(0, count - 1, up_step, last)
    keep = pltpu.make_async_copy(solved, solved_hbm, solved_sem)
    keep.start()
    message[lat, me] = send[me]
    to_pair(me, lat).start()

    load_zonal.wait()
    load_legendre.start()
    row = lax.broadcasted_iota(jnp.int32, (8, phi_count), 0)
    column = lax.broadcasted_iota(jnp.int32, (8, phi_count), 1).astype(F32)
    wave = jnp.zeros((8, phi_count), F32)
    for i in range(modes):
        wave = jnp.where(row == i, modes_ref[i].astype(F32), wave)
    turns = wave * column
    turns = turns - phi_count * jnp.floor((turns + 0.5) * (1.0 / phi_count))
    angle = turns * (2.0 * math.pi / phi_count)
    sine, cosine = jnp.sin(angle), jnp.cos(angle)
    factor = wave * (2.0 / degrees)
    slope = [(-factor * t).astype(BF16).astype(F32) for t in (sine, cosine)]
    turn = [(t * (2.0 / phi_count)).astype(BF16).astype(F32) for t in (cosine, -sine)]
    rows = []
    for c in range(2):
        for e in range(2):
            for i in range(modes):
                rows.append(slope[c if e == 0 else 1 - c][i : i + 1] * turn[c])
    table = jnp.concatenate(rows, 0)
    high = table.astype(BF16)
    rest = (table - high.astype(F32)).astype(BF16)
    tables = jnp.concatenate([high, rest], 0)
    across = (((1,), (1,)), ((), ()))
    pairs = 2 * modes * 8

    def azimuth(r):
        value = lax.dot_general(tables, zonal[r], across, preferred_element_type=F32)
        value = value[: 2 * pairs] + value[2 * pairs :]
        for c in range(2):
            for part in range(cycles // LANES):
                waves[part, pl.ds(c * levels + r, pairs, stride=8), :] = value[
                    c * pairs : (c + 1) * pairs, part * LANES : (part + 1) * LANES
                ]

    for r in range(levels // 2):
        azimuth(r)
    blocks.order(raw_slots, halves, slots)

    def heat(n, _):
        here = pl.ds(pl.multiple_of(n * LANES, LANES), LANES)
        low = slots[:, here] & (LOW - 1)
        rows = lax.broadcasted_iota(jnp.int32, (LOW, LANES), 0)
        hot[:, here] = jnp.where(rows == low, 1.0, 0.0).astype(BF16)
        return 0

    lax.fori_loop(0, halves * blocks.half // LANES, heat, 0)

    def lay(at, value):
        here = pl.ds(pl.multiple_of(at, LANES), LANES)
        high = lax.shift_right_arithmetic(slots[:, here], SHIFT)
        for h in range(0, high_count, 2):
            pair = [jnp.where(high == h + n, value, 0.0) for n in range(2)]
            spread[h * values : (h + 2) * values, here] = jnp.concatenate(pair, 0).astype(BF16)

    def lay_main(half, source):
        if blocks.full:
            lay(half * blocks.half + source * LANES, message[half, source].astype(F32)[:values])

    def lay_tails(half):
        share, slot = blocks.share, blocks.slot

        def step(group, _):
            sets = [
                message[half, group * share + d].astype(F32)[base : base + 8]
                for d in range(share)
            ]
            pieces = [
                jnp.concatenate([s[:, g * slot : (g + 1) * slot] for s in sets], 1)
                for g in range(blocks.groups)
            ]
            at = half * blocks.half + blocks.main + group * LANES
            lay(at, jnp.concatenate(pieces, 0))
            return 0

        lax.fori_loop(0, ranks // share, step, 0)

    def hand_on(d, _):
        source = lax.rem(me + ranks - d, ranks)
        to_rank(source, source).wait_recv()
        to_pair(source, lat).start()
        return 0

    lax.fori_loop(1, ranks, hand_on, 0)

    for r in range(levels // 2, levels):
        azimuth(r)

    def mine(source, _):
        lay_main(lat, source)
        return 0

    lax.fori_loop(0, ranks, mine, 0)
    lay_tails(lat)

    def theirs(source, _):
        to_pair(source, 1 - lat).wait_recv()
        lay_main(1 - lat, source)
        return 0

    lax.fori_loop(0, ranks, theirs, 0)
    lay_tails(1 - lat)

    coeffs = lax.dot_general(spread[...], hot[...], across, preferred_element_type=F32)
    lane = lax.broadcasted_iota(jnp.int32, (values, LOW), 1)

    def allowed(i, n):
        return lane + n * LOW >= modes_ref[i]

    load_legendre.wait()
    for i in range(modes):
        rows = []
        for n in range(chunks):
            at = (i * chunks + n) * values
            rows.append(jnp.where(allowed(i, n), coeffs[at : at + values], 0.0).astype(BF16))
        value = jnp.dot(jnp.concatenate(rows, 1), legendre[i], preferred_element_type=F32)
        value = value.astype(BF16).astype(F32)
        spectral[i] = value
        for f in range(fields):
            turned[i, f * 8 : f * 8 + 8] = pltpu.roll(value[f * 8 : f * 8 + 8], 4, 0)

    sums = []
    for j in range(modes):
        stack = []
        for f in range(fields):
            parts = []
            for part in range(cycles // LANES):
                acc = None
                for e, source in enumerate((spectral, turned)):
                    for i in range(modes):
                        at = ((e * modes + i) * 8 + j) * 8
                        term = (
                            source[i, f * 8 : f * 8 + 8, part * LANES : (part + 1) * LANES]
                            * waves[part, at : at + 8, :]
                        )
                        acc = term if acc is None else acc + term
                parts.append(acc)
            stack.append(jnp.concatenate(parts, 1))
        sums.append((jnp.concatenate(stack, 0) * weight[...][None, :]).astype(BF16))

    pieces = []
    for i in range(modes):
        value = lax.dot_general(sums[i], legendre[i], across, preferred_element_type=F32)
        for n in range(chunks):
            piece = value[:, n * LOW : (n + 1) * LOW]
            pieces.append(jnp.where(allowed(i, n), piece, 0.0))
    advection = jnp.concatenate(pieces, 0).astype(BF16)

    wide = 4 * LANES

    def collect(at):
        here = pl.ds(pl.multiple_of(at, LANES), wide)
        value = jnp.dot(advection, hot[:, here], preferred_element_type=F32)
        high = lax.shift_right_arithmetic(slots[:, here], SHIFT)
        acc = jnp.zeros((values, wide), F32)
        for h in range(high_count):
            acc = jnp.where(high == h, value[h * values : (h + 1) * values], acc)
        return acc

    def collect_half(half, handle):
        slot = blocks.slot
        many = wide // slot

        def tail_step(n, _):
            value = collect(half * blocks.half + blocks.main + n * wide)
            for d in range(many):
                tails[n * many + d] = blocks.lanes(
                    [
                        value[g * 8 : g * 8 + 8, d * slot : (d + 1) * slot]
                        for g in range(blocks.groups)
                    ]
                )
            return 0

        lax.fori_loop(0, ranks // many, tail_step, 0)

        if blocks.full:

            def main_step(n, _):
                turn = lax.rem(me // 4 + 1 + n, ranks // 4)
                value = collect(half * blocks.half + turn * wide)
                for u in range(4):
                    rank = turn * 4 + u
                    handle(
                        rank, blocks.join(value[:, u * LANES : (u + 1) * LANES], tails[rank])
                    )
                return 0

            lax.fori_loop(0, ranks // 4, main_step, 0)
        else:

            def rank_step(n, _):
                rank = lax.rem(me + 1 + n, ranks)
                handle(rank, blocks.join(None, tails[rank]))
                return 0

            lax.fori_loop(0, ranks, rank_step, 0)

    def pair_back(rank):
        return pltpu.make_async_remote_copy(
            src_ref=give.at[rank], dst_ref=other.at[rank],
            send_sem=pass2_sem.at[rank], recv_sem=got2_sem.at[rank],
            device_id=(me, 1 - lat), device_id_type=MESH,
        )

    def rank_back(rank, source):
        return pltpu.make_async_remote_copy(
            src_ref=total.at[rank], dst_ref=back.at[source],
            send_sem=send2_sem.at[rank], recv_sem=recv2_sem.at[source],
            device_id=(rank, lat), device_id_type=MESH,
        )

    def to_other(rank, block):
        give[rank] = block.astype(BF16)
        pair_back(rank).start()

    def to_owner(rank, block):
        pair_back(rank).wait_recv()
        total[rank] = (block + other[rank].astype(F32)).astype(BF16)

        @pl.when(rank != me)
        def _():
            rank_back(rank, me).start()

    collect_half(1 - lat, to_other)
    collect_half(lat, to_owner)
    back[me] = total[me]

    def sent(d, _):
        rank = lax.rem(me + d, ranks)
        to_rank(rank, me).wait_send()
        to_pair(rank, lat).wait_send()
        pair_back(rank).wait_send()
        return 0

    lax.fori_loop(1, ranks, sent, 0)
    to_pair(me, lat).wait_send()
    pair_back(me).wait_send()
    keep.wait()

    def arrived(d, _):
        source = lax.rem(me + ranks - d, ranks)
        rank_back(source, source).wait_recv()
        return 0

    lax.fori_loop(1, ranks, arrived, 0)

    def sent_back(d, _):
        rank_back(lax.rem(me + d, ranks), me).wait_send()
        return 0

    lax.fori_loop(1, ranks, sent_back, 0)


def last_kernel(
    blocks, spacing, back, solved, solved_out, out, held, passing, load_sem, solved_sem
):
    ranks, values, base = blocks.ranks, blocks.values, blocks.base
    items, depth, columns = out.shape
    levels = depth // ranks

    def load(item):
        return pltpu.make_async_copy(solved.at[item], passing.at[item], load_sem.at[item])

    def leave(item):
        return pltpu.make_async_copy(passing.at[item], solved_out.at[item], solved_sem.at[item])

    for item in range(items):
        load(item).start()
    edge = 8
    held[:, 0:edge, :] = jnp.zeros((items, edge, columns), F32)
    held[:, edge + depth : 2 * edge + depth, :] = jnp.zeros((items, edge, columns), F32)
    for rank in range(ranks):
        value = back[rank].astype(F32)
        tail = jnp.concatenate(
            [
                value[base : base + 8, g * blocks.slot : g * blocks.slot + blocks.tail]
                for g in range(blocks.groups)
            ],
            0,
        )
        at = edge + rank * levels
        for item in range(items):
            here = slice(item * levels, (item + 1) * levels)
            if blocks.full:
                held[item, at : at + levels, 0:LANES] = value[here]
            held[item, at : at + levels, blocks.full * LANES : columns] = tail[here]

    for item in range(items):
        load(item).wait()
        leave(item).start()
    keep = lax.broadcasted_iota(jnp.int32, (depth, depth), 0) == lax.broadcasted_iota(
        jnp.int32, (depth, depth), 1
    )
    scale = jnp.sum(jnp.where(keep, spacing[...][None, :], 0.0), axis=1, keepdims=True)
    for item in range(items):

        def shifted(n):
            return held[item, edge + n : edge + n + depth, :]

        slant = shifted(-2) - 8.0 * shifted(-1) + 8.0 * shifted(1) - shifted(2)
        out[item] = shifted(0) + scale * slant

    for item in range(items):
        leave(item).wait()


def body(
    forcing,
    pivots,
    lower,
    upper,
    slab_modes,
    slot_of_column,
    legendre,
    cycle_weight,
    zonal_flow,
    inverse_spacing,
):
    ranks, halves = lax.axis_size("rad"), lax.axis_size("lat")
    columns, depth = forcing.shape[2], forcing.shape[3]
    modes, degrees, cycles = legendre.shape
    levels = zonal_flow.shape[0]
    items = 6
    values = items * levels
    blocks = Blocks(columns, values, ranks)
    line = (ranks, blocks.rows, LANES)
    total = halves * blocks.half
    matrices = [m.transpose(1, 2, 3, 0) for m in (pivots, lower, upper)]
    right = forcing.transpose(0, 1, 3, 2).reshape(items, depth, columns)
    sizes = [right, *matrices, zonal_flow, legendre]

    grid = jax.ShapeDtypeStruct((items, depth, columns), F32)

    solved, back = pl.pallas_call(
        functools.partial(kernel, blocks, halves),
        out_shape=(grid, jax.ShapeDtypeStruct(line, BF16)),
        in_specs=[SMEM] + [VMEM] * 2 + [ANY] * 6,
        out_specs=(ANY, VMEM),
        scratch_shapes=[pltpu.VMEM((1, total), jnp.int32)]
        + [pltpu.VMEM(x.shape, x.dtype) for x in sizes]
        + [
            pltpu.VMEM((items, depth, columns), F32),
            pltpu.VMEM((ranks, values, columns), F32),
            pltpu.VMEM(line, BF16),
            pltpu.VMEM((halves,) + line, BF16),
            pltpu.VMEM((LOW, total), BF16),
            pltpu.VMEM((modes * (degrees // LOW) * values, total), BF16),
            pltpu.VMEM((cycles // LANES, 2 * modes * 8 * 8, LANES), F32),
            pltpu.VMEM((modes, values, cycles), F32),
            pltpu.VMEM((modes, values, cycles), F32),
            pltpu.VMEM((ranks, 8, LANES), F32),
            pltpu.VMEM(line, BF16),
            pltpu.VMEM(line, BF16),
            pltpu.VMEM(line, BF16),
            pltpu.SemaphoreType.DMA((7,)),
            pltpu.SemaphoreType.DMA,
        ]
        + [pltpu.SemaphoreType.DMA((ranks,))] * 8,
        compiler_params=pltpu.CompilerParams(
            vmem_limit_bytes=ROOM, collective_id=0, has_side_effects=True
        ),
        name="step",
    )(slab_modes, slot_of_column, cycle_weight, right, *matrices, zonal_flow, legendre)

    solved, explicit = pl.pallas_call(
        functools.partial(last_kernel, blocks),
        out_shape=(grid, grid),
        in_specs=[VMEM, VMEM, ANY],
        out_specs=(ANY, VMEM),
        scratch_shapes=[
            pltpu.VMEM((items, depth + 16, columns), F32),
            pltpu.VMEM((items, depth, columns), F32),
            pltpu.SemaphoreType.DMA((items,)),
            pltpu.SemaphoreType.DMA((items,)),
        ],
        compiler_params=pltpu.CompilerParams(vmem_limit_bytes=ROOM),
        name="stencil",
    )(inverse_spacing, back, solved)

    def placed(value):
        return value.reshape(3, 2, depth, columns).transpose(0, 1, 3, 2)

    return (placed(solved), placed(explicit))


def solution(mesh):
    placed = (
        P(None, None, ("rad", "lat"), None),
        P(("rad", "lat"), None, None, None),
        P(("rad", "lat"), None, None, None),
        P(("rad", "lat"), None, None, None),
        P(),
        P(),
        P(None, None, "lat"),
        P("lat"),
        P("rad", "lat", None),
        P(),
    )
    return jax.shard_map(
        body,
        mesh=mesh,
        in_specs=placed,
        out_specs=(P(None, None, ("rad", "lat"), None), P(None, None, ("rad", "lat"), None)),
        check_vma=False,
    )
```

```python
import functools
import math

import jax
import jax.numpy as jnp
from jax import lax
from jax.experimental import pallas as pl
from jax.experimental.pallas import tpu as pltpu
from jax.sharding import PartitionSpec as P

LANES = 128
SHIFT = 8
LOW = 1 << SHIFT
MESH = pl.DeviceIdType.MESH
VMEM = pl.BlockSpec(memory_space=pltpu.VMEM)
SMEM = pl.BlockSpec(memory_space=pltpu.SMEM)
HBM = pl.BlockSpec(memory_space=pltpu.HBM)
F32 = jnp.float32
BF16 = jnp.bfloat16
MIB = 1024 * 1024


class Blocks:
    def __init__(self, columns, values, ranks):
        self.columns, self.values, self.ranks = columns, values, ranks
        self.full, self.tail = divmod(columns, LANES)
        self.groups = values // 8
        self.slot = 8
        while self.slot < self.tail:
            self.slot *= 2
        assert self.full <= 1 and self.slot * self.groups <= LANES
        self.base = self.full * values
        self.rows = -(-(self.base + 8) // 16) * 16
        self.share = LANES // self.slot
        self.main = ranks * self.full * LANES
        self.half = self.main + ranks * self.slot

    def join(self, main, tail):
        parts = ([main] if self.full else []) + [tail]
        spare = self.rows - self.base - 8
        if spare:
            parts.append(jnp.zeros((spare, LANES), tail.dtype))
        return jnp.concatenate(parts, 0)

    def lanes(self, pieces):
        parts = []
        for piece in pieces:
            parts.append(piece)
            if piece.shape[1] < self.slot:
                parts.append(jnp.zeros((8, self.slot - piece.shape[1]), piece.dtype))
        spare = LANES - self.slot * len(pieces)
        if spare:
            parts.append(jnp.zeros((8, spare), pieces[0].dtype))
        return jnp.concatenate(parts, 1)

    def pack(self, value):
        rest = value[:, self.full * LANES :]
        tail = self.lanes([rest[8 * g : 8 * g + 8] for g in range(self.groups)])
        return self.join(value[:, : self.full * LANES], tail)

    def order(self, raw, halves, slots):
        table = raw[...][None, :]
        for half in range(halves):
            for rank in range(self.ranks):
                at = (rank * halves + half) * self.columns
                if self.full:
                    here = half * self.half + rank * LANES
                    slots[:, here : here + LANES] = table[:, at : at + LANES]
                    at += LANES
            for first in range(0, self.ranks, self.share):
                parts = []
                for rank in range(first, first + self.share):
                    at = (rank * halves + half) * self.columns + self.full * LANES
                    parts.append(table[:, at : at + self.tail])
                    if self.slot > self.tail:
                        parts.append(jnp.full((1, self.slot - self.tail), -1, jnp.int32))
                here = half * self.half + self.main + first * self.slot
                slots[:, here : here + LANES] = jnp.concatenate(parts, 1)


def sublane_sums(values):
    row = lax.broadcasted_iota(jnp.int32, values[0].shape, 0)
    step = 1
    while len(values) > 1:
        keep = (row & step) == 0
        merged = []
        for first, second in zip(values[0::2], values[1::2]):
            straight = jnp.where(keep, first, second)
            crossed = jnp.where(keep, second, first)
            merged.append(straight + pltpu.roll(crossed, step, 0))
        values, step = merged, step * 2
    return values[0]


def kernel(
    blocks, halves, modes_ref, slots_hbm, weight_hbm, forcing_hbm, pivots_hbm, lower_hbm,
    upper_hbm, zonal_hbm, legendre_hbm, solved, back,
    raw_slots, weight, slots, forcing, pivots, lower, upper, zonal, legendre, stage, send, message, hot, spread,
    waves, spectral, turned, tails, give, other, total, tables,
    load_sem, send_sem, recv_sem, pass_sem, got_sem,
    send2_sem, recv2_sem, pass2_sem, got2_sem,
):
    me, lat = lax.axis_index("rad"), lax.axis_index("lat")
    ranks, values, base = blocks.ranks, blocks.values, blocks.base
    items, depth, columns = forcing.shape
    count, size = pivots.shape[0], pivots.shape[1]
    levels = depth // ranks
    modes, degrees, cycles = legendre.shape
    phi_count = zonal.shape[2]
    chunks = degrees // LOW
    high_count = modes * chunks
    fields = values // 8

    def load(n, source, target):
        return pltpu.make_async_copy(source, target, load_sem.at[n])

    load_right = load(0, forcing_hbm, forcing)
    load_first = load(1, pivots_hbm.at[0], pivots.at[0])
    load_rest = load(2, pivots_hbm.at[pl.ds(1, count - 1)], pivots.at[pl.ds(1, count - 1)])
    load_lower = load(3, lower_hbm, lower)
    load_upper = load(4, upper_hbm, upper)
    load_zonal = load(5, zonal_hbm, zonal)
    load_legendre = load(6, legendre_hbm, legendre)
    load_slots = load(7, slots_hbm, raw_slots)
    load_weight = load(8, weight_hbm, weight)
    for one in (load_right, load_first, load_lower, load_rest, load_upper):
        one.start()
    load_slots.start()
    load_weight.start()

    barrier = pltpu.get_barrier_semaphore()
    pl.semaphore_signal(barrier, inc=1, device_id=(me, 1 - lat), device_id_type=MESH)

    def hello(d, _):
        rank = lax.rem(me + d, ranks)
        pl.semaphore_signal(barrier, inc=1, device_id=(rank, lat), device_id_type=MESH)
        return 0

    lax.fori_loop(1, ranks, hello, 0)

    def to_rank(rank, source):
        return pltpu.make_async_remote_copy(
            src_ref=send.at[rank], dst_ref=message.at[lat, source],
            send_sem=send_sem.at[rank], recv_sem=recv_sem.at[source],
            device_id=(rank, lat), device_id_type=MESH,
        )

    def to_pair(source, half):
        return pltpu.make_async_remote_copy(
            src_ref=message.at[lat, source], dst_ref=message.at[half, source],
            send_sem=pass_sem.at[source], recv_sem=got_sem.at[source],
            device_id=(me, 1 - lat), device_id_type=MESH,
        )

    def apply_block(matrix, at, vectors):
        pieces = [[] for _ in vectors]
        for i in range(0, size, 8):
            for item, vector in enumerate(vectors):
                sums = []
                for n in range(8):
                    acc = matrix[at, i + n, 0:8] * vector[0:8]
                    for j in range(8, size, 8):
                        acc = acc + matrix[at, i + n, j : j + 8] * vector[j : j + 8]
                    sums.append(acc)
                pieces[item].append(sublane_sums(sums))
        return [jnp.concatenate(p, 0) for p in pieces]

    def span(k):
        return pl.ds(k * size if isinstance(k, int) else pl.multiple_of(k * size, size), size)

    per_block = size // levels

    def emit(k, vectors):
        for u in range(per_block):
            for item in range(items):
                stage[k * per_block + u, item * levels : (item + 1) * levels, :] = vectors[item][
                    u * levels : (u + 1) * levels
                ]

        def give_one(u, _):
            rank = k * per_block + u
            send[rank] = blocks.pack(stage[rank]).astype(BF16)

            @pl.when(rank != me)
            def _():
                to_rank(rank, me).start()

            return 0

        lax.fori_loop(0, per_block, give_one, 0)

    row = lax.broadcasted_iota(jnp.int32, (8, phi_count), 0)
    column = lax.broadcasted_iota(jnp.int32, (8, phi_count), 1).astype(F32)
    wave = jnp.zeros((8, phi_count), F32)
    for i in range(modes):
        wave = jnp.where(row == i, modes_ref[i].astype(F32), wave)
    turns = wave * column
    turns = turns - phi_count * jnp.floor((turns + 0.5) * (1.0 / phi_count))
    angle = turns * (2.0 * math.pi / phi_count)
    sine, cosine = jnp.sin(angle), jnp.cos(angle)
    factor = wave * (2.0 / degrees)
    slope = [(-factor * t).astype(BF16).astype(F32) for t in (sine, cosine)]
    turn = [(t * (2.0 / phi_count)).astype(BF16).astype(F32) for t in (cosine, -sine)]
    rows = []
    for c in range(2):
        for e in range(2):
            for i in range(modes):
                rows.append(slope[c if e == 0 else 1 - c][i : i + 1] * turn[c])
    table = jnp.concatenate(rows, 0)
    tables[...] = table.astype(BF16)

    load_right.wait()
    load_first.wait()
    first = apply_block(pivots, 0, [forcing[item, span(0)] for item in range(items)])
    for item in range(items):
        solved[item, span(0)] = first[item]
    load_lower.wait()
    load_rest.wait()
    load_zonal.start()

    def descend(k, carry):
        drop = apply_block(lower, k - 1, carry)
        rest = [forcing[item, span(k)] - drop[item] for item in range(items)]
        now = apply_block(pivots, k, rest)
        for item in range(items):
            solved[item, span(k)] = now[item]
        return tuple(now)

    last = tuple(first)
    if count == 2:
        last = descend(1, last)
    else:
        last = lax.fori_loop(1, count, descend, last)
    load_upper.wait()
    pl.semaphore_wait(barrier, ranks)
    emit(count - 1, last)

    def up_step(step, carry):
        k = count - 2 - step
        drop = apply_block(upper, k, carry)
        now = [solved[item, span(k)] - drop[item] for item in range(items)]
        for item in range(items):
            solved[item, span(k)] = now[item]
        emit(k, now)
        return tuple(now)

    if count == 2:
        up_step(0, last)
    else:
        lax.fori_loop(0, count - 1, up_step, last)
    message[lat, me] = send[me]
    to_pair(me, lat).start()

    load_zonal.wait()
    load_legendre.start()
    across = (((1,), (1,)), ((), ()))
    pairs = 2 * modes * 8

    def azimuth(r):
        flow = zonal[r : r + 2].reshape(2 * cycles, phi_count)
        value = lax.dot_general(tables[...], flow, across, preferred_element_type=F32)
        for u in range(2):
            for c in range(2):
                for part in range(cycles // LANES):
                    at = u * cycles + part * LANES
                    waves[part, pl.ds(c * levels + r + u, pairs, stride=8), :] = value[
                        c * pairs : (c + 1) * pairs, at : at + LANES
                    ]

    for r in range(0, levels // 2, 2):
        azimuth(r)
    load_slots.wait()
    blocks.order(raw_slots, halves, slots)

    def heat(n, _):
        here = pl.ds(pl.multiple_of(n * LANES, LANES), LANES)
        low = slots[:, here] & (LOW - 1)
        rows = lax.broadcasted_iota(jnp.int32, (LOW, LANES), 0)
        hot[:, here] = jnp.where(rows == low, 1.0, 0.0).astype(BF16)
        return 0

    lax.fori_loop(0, halves * blocks.half // LANES, heat, 0)

    def lay(at, value):
        here = pl.ds(pl.multiple_of(at, LANES), LANES)
        high = lax.shift_right_arithmetic(slots[:, here], SHIFT)
        for h in range(0, high_count, 2):
            pair = [jnp.where(high == h + n, value, 0.0) for n in range(2)]
            spread[h * values : (h + 2) * values, here] = jnp.concatenate(pair, 0).astype(BF16)

    def lay_main(half, source):
        if blocks.full:
            lay(half * blocks.half + source * LANES, message[half, source].astype(F32)[:values])

    def lay_tails(half):
        share, slot = blocks.share, blocks.slot

        def step(group, _):
            sets = [
                message[half, group * share + d].astype(F32)[base : base + 8]
                for d in range(share)
            ]
            pieces = [
                jnp.concatenate([s[:, g * slot : (g + 1) * slot] for s in sets], 1)
                for g in range(blocks.groups)
            ]
            at = half * blocks.half + blocks.main + group * LANES
            lay(at, jnp.concatenate(pieces, 0))
            return 0

        lax.fori_loop(0, ranks // share, step, 0)

    def hand_on(d, _):
        source = lax.rem(me + ranks - d, ranks)
        to_rank(source, source).wait_recv()
        to_pair(source, lat).start()
        return 0

    lax.fori_loop(1, ranks, hand_on, 0)

    for r in range(levels // 2, levels, 2):
        azimuth(r)

    def mine(source, _):
        lay_main(lat, source)
        return 0

    lax.fori_loop(0, ranks, mine, 0)
    lay_tails(lat)

    def theirs(source, _):
        to_pair(source, 1 - lat).wait_recv()
        lay_main(1 - lat, source)
        return 0

    lax.fori_loop(0, ranks, theirs, 0)
    lay_tails(1 - lat)

    coeffs = lax.dot_general(spread[...], hot[...], across, preferred_element_type=F32)
    lane = lax.broadcasted_iota(jnp.int32, (values, LOW), 1)

    def allowed(i, n):
        return lane + n * LOW >= modes_ref[i]

    load_legendre.wait()
    load_weight.wait()
    for i in range(modes):
        rows = []
        for n in range(chunks):
            at = (i * chunks + n) * values
            rows.append(jnp.where(allowed(i, n), coeffs[at : at + values], 0.0).astype(BF16))
        value = jnp.dot(jnp.concatenate(rows, 1), legendre[i], preferred_element_type=F32)
        value = value.astype(BF16).astype(F32)
        spectral[i] = value
        for f in range(fields):
            turned[i, f * 8 : f * 8 + 8] = pltpu.roll(value[f * 8 : f * 8 + 8], 4, 0)

    sums = []
    for j in range(modes):
        stack = []
        for f in range(fields):
            parts = []
            for part in range(cycles // LANES):
                acc = None
                for e, source in enumerate((spectral, turned)):
                    for i in range(modes):
                        at = ((e * modes + i) * 8 + j) * 8
                        term = (
                            source[i, f * 8 : f * 8 + 8, part * LANES : (part + 1) * LANES]
                            * waves[part, at : at + 8, :]
                        )
                        acc = term if acc is None else acc + term
                parts.append(acc)
            stack.append(jnp.concatenate(parts, 1))
        sums.append((jnp.concatenate(stack, 0) * weight[...][None, :]).astype(BF16))

    pieces = []
    for i in range(modes):
        value = lax.dot_general(sums[i], legendre[i], across, preferred_element_type=F32)
        for n in range(chunks):
            piece = value[:, n * LOW : (n + 1) * LOW]
            pieces.append(jnp.where(allowed(i, n), piece, 0.0))
    advection = jnp.concatenate(pieces, 0).astype(BF16)

    wide = 4 * LANES

    def collect(at):
        here = pl.ds(pl.multiple_of(at, LANES), wide)
        value = jnp.dot(advection, hot[:, here], preferred_element_type=F32)
        high = lax.shift_right_arithmetic(slots[:, here], SHIFT)
        acc = jnp.zeros((values, wide), F32)
        for h in range(high_count):
            acc = jnp.where(high == h, value[h * values : (h + 1) * values], acc)
        return acc

    def collect_half(half, handle):
        slot = blocks.slot
        many = wide // slot

        def tail_step(n, _):
            value = collect(half * blocks.half + blocks.main + n * wide)
            for d in range(many):
                tails[n * many + d] = blocks.lanes(
                    [
                        value[g * 8 : g * 8 + 8, d * slot : (d + 1) * slot]
                        for g in range(blocks.groups)
                    ]
                )
            return 0

        lax.fori_loop(0, ranks // many, tail_step, 0)

        if blocks.full:

            def main_step(n, _):
                turn = lax.rem(me // 4 + 1 + n, ranks // 4)
                value = collect(half * blocks.half + turn * wide)
                for u in range(4):
                    rank = turn * 4 + u
                    handle(
                        rank, blocks.join(value[:, u * LANES : (u + 1) * LANES], tails[rank])
                    )
                return 0

            lax.fori_loop(0, ranks // 4, main_step, 0)
        else:

            def rank_step(n, _):
                rank = lax.rem(me + 1 + n, ranks)
                handle(rank, blocks.join(None, tails[rank]))
                return 0

            lax.fori_loop(0, ranks, rank_step, 0)

    def pair_back(rank):
        return pltpu.make_async_remote_copy(
            src_ref=give.at[rank], dst_ref=other.at[rank],
            send_sem=pass2_sem.at[rank], recv_sem=got2_sem.at[rank],
            device_id=(me, 1 - lat), device_id_type=MESH,
        )

    def rank_back(rank, source):
        return pltpu.make_async_remote_copy(
            src_ref=total.at[rank], dst_ref=back.at[source],
            send_sem=send2_sem.at[rank], recv_sem=recv2_sem.at[source],
            device_id=(rank, lat), device_id_type=MESH,
        )

    def to_other(rank, block):
        give[rank] = block.astype(BF16)
        pair_back(rank).start()

    def to_owner(rank, block):
        pair_back(rank).wait_recv()
        total[rank] = (block + other[rank].astype(F32)).astype(BF16)

        @pl.when(rank != me)
        def _():
            rank_back(rank, me).start()

    collect_half(1 - lat, to_other)
    collect_half(lat, to_owner)
    back[me] = total[me]

    def sent(d, _):
        rank = lax.rem(me + d, ranks)
        to_rank(rank, me).wait_send()
        to_pair(rank, lat).wait_send()
        pair_back(rank).wait_send()
        return 0

    lax.fori_loop(1, ranks, sent, 0)
    to_pair(me, lat).wait_send()
    pair_back(me).wait_send()

    def arrived(d, _):
        source = lax.rem(me + ranks - d, ranks)
        rank_back(source, source).wait_recv()
        return 0

    lax.fori_loop(1, ranks, arrived, 0)

    def sent_back(d, _):
        rank_back(lax.rem(me + d, ranks), me).wait_send()
        return 0

    lax.fori_loop(1, ranks, sent_back, 0)


def last_kernel(
    blocks, spacing, back, solved, solved_out, out, held, solved_sem
):
    ranks, values, base = blocks.ranks, blocks.values, blocks.base
    items, depth, columns = out.shape
    levels = depth // ranks

    hand_on = pltpu.make_async_copy(solved, solved_out, solved_sem)
    hand_on.start()
    edge = 8
    held[:, 0:edge, :] = jnp.zeros((items, edge, columns), F32)
    held[:, edge + depth : 2 * edge + depth, :] = jnp.zeros((items, edge, columns), F32)
    for rank in range(ranks):
        value = back[rank].astype(F32)
        tail = jnp.concatenate(
            [
                value[base : base + 8, g * blocks.slot : g * blocks.slot + blocks.tail]
                for g in range(blocks.groups)
            ],
            0,
        )
        at = edge + rank * levels
        for item in range(items):
            here = slice(item * levels, (item + 1) * levels)
            if blocks.full:
                held[item, at : at + levels, 0:LANES] = value[here]
            held[item, at : at + levels, blocks.full * LANES : columns] = tail[here]

    keep = lax.broadcasted_iota(jnp.int32, (depth, depth), 0) == lax.broadcasted_iota(
        jnp.int32, (depth, depth), 1
    )
    scale = jnp.sum(jnp.where(keep, spacing[...][None, :], 0.0), axis=1, keepdims=True)
    for item in range(items):

        def shifted(n):
            return held[item, edge + n : edge + n + depth, :]

        slant = shifted(-2) - 8.0 * shifted(-1) + 8.0 * shifted(1) - shifted(2)
        out[item] = shifted(0) + scale * slant

    hand_on.wait()


def body(
    forcing,
    pivots,
    lower,
    upper,
    slab_modes,
    slot_of_column,
    legendre,
    cycle_weight,
    zonal_flow,
    inverse_spacing,
):
    ranks, halves = lax.axis_size("rad"), lax.axis_size("lat")
    columns, depth = forcing.shape[2], forcing.shape[3]
    modes, degrees, cycles = legendre.shape
    levels = zonal_flow.shape[0]
    items = 6
    values = items * levels
    blocks = Blocks(columns, values, ranks)
    line = (ranks, blocks.rows, LANES)
    total = halves * blocks.half
    matrices = [m.transpose(1, 2, 3, 0) for m in (pivots, lower, upper)]
    right = forcing.transpose(0, 1, 3, 2).reshape(items, depth, columns)
    sizes = [right, *matrices, zonal_flow, legendre]

    grid = jax.ShapeDtypeStruct((items, depth, columns), F32)

    solved, back = pl.pallas_call(
        functools.partial(kernel, blocks, halves),
        out_shape=(grid, jax.ShapeDtypeStruct(line, BF16)),
        in_specs=[SMEM] + [HBM] * 8,
        out_specs=(VMEM, VMEM),
        scratch_shapes=[
            pltpu.VMEM(slot_of_column.shape, jnp.int32),
            pltpu.VMEM(cycle_weight.shape, F32),
            pltpu.VMEM((1, total), jnp.int32),
        ]
        + [pltpu.VMEM(x.shape, x.dtype) for x in sizes]
        + [
            pltpu.VMEM((ranks, values, columns), F32),
            pltpu.VMEM(line, BF16),
            pltpu.VMEM((halves,) + line, BF16),
            pltpu.VMEM((LOW, total), BF16),
            pltpu.VMEM((modes * (degrees // LOW) * values, total), BF16),
            pltpu.VMEM((cycles // LANES, 2 * modes * 8 * 8, LANES), F32),
            pltpu.VMEM((modes, values, cycles), F32),
            pltpu.VMEM((modes, values, cycles), F32),
            pltpu.VMEM((ranks, 8, LANES), F32),
            pltpu.VMEM(line, BF16),
            pltpu.VMEM(line, BF16),
            pltpu.VMEM(line, BF16),
            pltpu.VMEM((4 * modes * 8, zonal_flow.shape[2]), BF16),
            pltpu.SemaphoreType.DMA((9,)),
        ]
        + [pltpu.SemaphoreType.DMA((ranks,))] * 8,
        compiler_params=pltpu.CompilerParams(
            vmem_limit_bytes=(53 if total <= 8000 else 60) * MIB, collective_id=0, has_side_effects=True
        ),
        name="step",
    )(slab_modes, slot_of_column, cycle_weight, right, *matrices, zonal_flow, legendre)

    solved, explicit = pl.pallas_call(
        functools.partial(last_kernel, blocks),
        out_shape=(grid, grid),
        in_specs=[VMEM] * 3,
        out_specs=(HBM, VMEM),
        scratch_shapes=[
            pltpu.VMEM((items, depth + 16, columns), F32),
            pltpu.SemaphoreType.DMA,
        ],
        compiler_params=pltpu.CompilerParams(vmem_limit_bytes=16 * MIB),
        name="stencil",
    )(inverse_spacing, back, solved)

    def placed(value):
        return value.reshape(3, 2, depth, columns).transpose(0, 1, 3, 2)

    return (placed(solved), placed(explicit))


def solution(mesh):
    placed = (
        P(None, None, ("rad", "lat"), None),
        P(("rad", "lat"), None, None, None),
        P(("rad", "lat"), None, None, None),
        P(("rad", "lat"), None, None, None),
        P(),
        P(),
        P(None, None, "lat"),
        P("lat"),
        P("rad", "lat", None),
        P(),
    )
    return jax.shard_map(
        body,
        mesh=mesh,
        in_specs=placed,
        out_specs=(P(None, None, ("rad", "lat"), None), P(None, None, ("rad", "lat"), None)),
        check_vma=False,
    )
```

```python
import functools
import math

import jax
import jax.numpy as jnp
from jax import lax
from jax.experimental import pallas as pl
from jax.experimental.pallas import tpu as pltpu
from jax.sharding import PartitionSpec as P

LANES = 128
SHIFT = 8
LOW = 1 << SHIFT
MESH = pl.DeviceIdType.MESH
VMEM = pl.BlockSpec(memory_space=pltpu.VMEM)
SMEM = pl.BlockSpec(memory_space=pltpu.SMEM)
HBM = pl.BlockSpec(memory_space=pltpu.HBM)
F32 = jnp.float32
BF16 = jnp.bfloat16
MIB = 1024 * 1024


class Blocks:
    def __init__(self, columns, values, ranks):
        self.columns, self.values, self.ranks = columns, values, ranks
        self.full, self.tail = divmod(columns, LANES)
        self.groups = values // 8
        self.slot = 8
        while self.slot < self.tail:
            self.slot *= 2
        assert self.full <= 1 and self.slot * self.groups <= LANES
        self.base = self.full * values
        self.rows = -(-(self.base + 8) // 16) * 16
        self.share = LANES // self.slot
        self.main = ranks * self.full * LANES
        self.half = self.main + ranks * self.slot

    def join(self, main, tail):
        parts = ([main] if self.full else []) + [tail]
        spare = self.rows - self.base - 8
        if spare:
            parts.append(jnp.zeros((spare, LANES), tail.dtype))
        return jnp.concatenate(parts, 0)

    def lanes(self, pieces):
        parts = []
        for piece in pieces:
            parts.append(piece)
            if piece.shape[1] < self.slot:
                parts.append(jnp.zeros((8, self.slot - piece.shape[1]), piece.dtype))
        spare = LANES - self.slot * len(pieces)
        if spare:
            parts.append(jnp.zeros((8, spare), pieces[0].dtype))
        return jnp.concatenate(parts, 1)

    def pack(self, value):
        rest = value[:, self.full * LANES :]
        tail = self.lanes([rest[8 * g : 8 * g + 8] for g in range(self.groups)])
        return self.join(value[:, : self.full * LANES], tail)

    def order(self, raw, halves, slots):
        table = raw[...][None, :]
        for half in range(halves):
            for rank in range(self.ranks):
                at = (rank * halves + half) * self.columns
                if self.full:
                    here = half * self.half + rank * LANES
                    slots[:, here : here + LANES] = table[:, at : at + LANES]
                    at += LANES
            for first in range(0, self.ranks, self.share):
                parts = []
                for rank in range(first, first + self.share):
                    at = (rank * halves + half) * self.columns + self.full * LANES
                    parts.append(table[:, at : at + self.tail])
                    if self.slot > self.tail:
                        parts.append(jnp.full((1, self.slot - self.tail), -1, jnp.int32))
                here = half * self.half + self.main + first * self.slot
                slots[:, here : here + LANES] = jnp.concatenate(parts, 1)


def sublane_sums(values):
    row = lax.broadcasted_iota(jnp.int32, values[0].shape, 0)
    step = 1
    while len(values) > 1:
        keep = (row & step) == 0
        merged = []
        for first, second in zip(values[0::2], values[1::2]):
            straight = jnp.where(keep, first, second)
            crossed = jnp.where(keep, second, first)
            merged.append(straight + pltpu.roll(crossed, step, 0))
        values, step = merged, step * 2
    return values[0]


def kernel(
    blocks, halves, modes_ref, slots_hbm, weight_hbm, forcing_hbm, pivots_hbm, lower_hbm,
    upper_hbm, zonal_hbm, legendre_hbm, solved_hbm, back,
    solved, raw_slots, weight, slots, forcing, pivots, lower, upper, zonal, legendre, stage, send, message, hot, spread,
    waves, spectral, turned, tails, give, other, total, tables,
    load_sem, send_sem, recv_sem, pass_sem, got_sem,
    send2_sem, recv2_sem, pass2_sem, got2_sem,
):
    me, lat = lax.axis_index("rad"), lax.axis_index("lat")
    ranks, values, base = blocks.ranks, blocks.values, blocks.base
    items, depth, columns = forcing.shape
    count, size = pivots.shape[0], pivots.shape[1]
    levels = depth // ranks
    modes, degrees, cycles = legendre.shape
    phi_count = zonal.shape[2]
    chunks = degrees // LOW
    high_count = modes * chunks
    fields = values // 8

    def load(n, source, target):
        return pltpu.make_async_copy(source, target, load_sem.at[n])

    load_right = load(0, forcing_hbm, forcing)
    load_first = load(1, pivots_hbm.at[0], pivots.at[0])
    load_rest = load(2, pivots_hbm.at[pl.ds(1, count - 1)], pivots.at[pl.ds(1, count - 1)])
    load_lower = load(3, lower_hbm, lower)
    load_upper = load(4, upper_hbm, upper)
    load_zonal = load(5, zonal_hbm, zonal)
    load_legendre = load(6, legendre_hbm, legendre)
    load_slots = load(7, slots_hbm, raw_slots)
    load_weight = load(8, weight_hbm, weight)
    for one in (load_right, load_first, load_lower, load_rest, load_upper):
        one.start()
    load_slots.start()
    load_weight.start()

    barrier = pltpu.get_barrier_semaphore()
    pl.semaphore_signal(barrier, inc=1, device_id=(me, 1 - lat), device_id_type=MESH)

    def hello(d, _):
        rank = lax.rem(me + d, ranks)
        pl.semaphore_signal(barrier, inc=1, device_id=(rank, lat), device_id_type=MESH)
        return 0

    lax.fori_loop(1, ranks, hello, 0)

    def to_rank(rank, source):
        return pltpu.make_async_remote_copy(
            src_ref=send.at[rank], dst_ref=message.at[lat, source],
            send_sem=send_sem.at[rank], recv_sem=recv_sem.at[source],
            device_id=(rank, lat), device_id_type=MESH,
        )

    def to_pair(source, half):
        return pltpu.make_async_remote_copy(
            src_ref=message.at[lat, source], dst_ref=message.at[half, source],
            send_sem=pass_sem.at[source], recv_sem=got_sem.at[source],
            device_id=(me, 1 - lat), device_id_type=MESH,
        )

    def apply_block(matrix, at, vectors):
        pieces = [[] for _ in vectors]
        for i in range(0, size, 8):
            for item, vector in enumerate(vectors):
                sums = []
                for n in range(8):
                    acc = matrix[at, i + n, 0:8] * vector[0:8]
                    for j in range(8, size, 8):
                        acc = acc + matrix[at, i + n, j : j + 8] * vector[j : j + 8]
                    sums.append(acc)
                pieces[item].append(sublane_sums(sums))
        return [jnp.concatenate(p, 0) for p in pieces]

    def span(k):
        return pl.ds(k * size if isinstance(k, int) else pl.multiple_of(k * size, size), size)

    per_block = size // levels

    def emit(k, vectors):
        for u in range(per_block):
            for item in range(items):
                stage[k * per_block + u, item * levels : (item + 1) * levels, :] = vectors[item][
                    u * levels : (u + 1) * levels
                ]

        def give_one(u, _):
            rank = k * per_block + u
            send[rank] = blocks.pack(stage[rank]).astype(BF16)

            @pl.when(rank != me)
            def _():
                to_rank(rank, me).start()

            return 0

        lax.fori_loop(0, per_block, give_one, 0)

    row = lax.broadcasted_iota(jnp.int32, (8, phi_count), 0)
    column = lax.broadcasted_iota(jnp.int32, (8, phi_count), 1).astype(F32)
    wave = jnp.zeros((8, phi_count), F32)
    for i in range(modes):
        wave = jnp.where(row == i, modes_ref[i].astype(F32), wave)
    turns = wave * column
    turns = turns - phi_count * jnp.floor((turns + 0.5) * (1.0 / phi_count))
    angle = turns * (2.0 * math.pi / phi_count)
    sine, cosine = jnp.sin(angle), jnp.cos(angle)
    factor = wave * (2.0 / degrees)
    slope = [(-factor * t).astype(BF16).astype(F32) for t in (sine, cosine)]
    turn = [(t * (2.0 / phi_count)).astype(BF16).astype(F32) for t in (cosine, -sine)]
    rows = []
    for c in range(2):
        for e in range(2):
            for i in range(modes):
                rows.append(slope[c if e == 0 else 1 - c][i : i + 1] * turn[c])
    table = jnp.concatenate(rows, 0)
    tables[...] = table.astype(BF16)

    load_right.wait()
    load_first.wait()
    first = apply_block(pivots, 0, [forcing[item, span(0)] for item in range(items)])
    for item in range(items):
        solved[item, span(0)] = first[item]
    load_lower.wait()
    load_rest.wait()
    load_zonal.start()

    def descend(k, carry):
        drop = apply_block(lower, k - 1, carry)
        rest = [forcing[item, span(k)] - drop[item] for item in range(items)]
        now = apply_block(pivots, k, rest)
        for item in range(items):
            solved[item, span(k)] = now[item]
        return tuple(now)

    last = tuple(first)
    if count == 2:
        last = descend(1, last)
    else:
        last = lax.fori_loop(1, count, descend, last)
    load_upper.wait()
    pl.semaphore_wait(barrier, ranks)
    emit(count - 1, last)

    def up_step(step, carry):
        k = count - 2 - step
        drop = apply_block(upper, k, carry)
        now = [solved[item, span(k)] - drop[item] for item in range(items)]
        for item in range(items):
            solved[item, span(k)] = now[item]
        emit(k, now)
        return tuple(now)

    if count == 2:
        up_step(0, last)
    else:
        lax.fori_loop(0, count - 1, up_step, last)
    keep = load(9, solved, solved_hbm)
    keep.start()
    message[lat, me] = send[me]
    to_pair(me, lat).start()

    load_zonal.wait()
    load_legendre.start()
    across = (((1,), (1,)), ((), ()))
    pairs = 2 * modes * 8

    def azimuth(r):
        flow = zonal[r : r + 2].reshape(2 * cycles, phi_count)
        value = lax.dot_general(tables[...], flow, across, preferred_element_type=F32)
        for u in range(2):
            for c in range(2):
                for part in range(cycles // LANES):
                    at = u * cycles + part * LANES
                    waves[part, pl.ds(c * levels + r + u, pairs, stride=8), :] = value[
                        c * pairs : (c + 1) * pairs, at : at + LANES
                    ]

    for r in range(0, levels // 2, 2):
        azimuth(r)
    load_slots.wait()
    blocks.order(raw_slots, halves, slots)

    def heat(n, _):
        here = pl.ds(pl.multiple_of(n * LANES, LANES), LANES)
        low = slots[:, here] & (LOW - 1)
        rows = lax.broadcasted_iota(jnp.int32, (LOW, LANES), 0)
        hot[:, here] = jnp.where(rows == low, 1.0, 0.0).astype(BF16)
        return 0

    lax.fori_loop(0, halves * blocks.half // LANES, heat, 0)

    def lay(at, value):
        here = pl.ds(pl.multiple_of(at, LANES), LANES)
        high = lax.shift_right_arithmetic(slots[:, here], SHIFT)
        for h in range(0, high_count, 2):
            pair = [jnp.where(high == h + n, value, 0.0) for n in range(2)]
            spread[h * values : (h + 2) * values, here] = jnp.concatenate(pair, 0).astype(BF16)

    def lay_main(half, source):
        if blocks.full:
            lay(half * blocks.half + source * LANES, message[half, source].astype(F32)[:values])

    def lay_tails(half):
        share, slot = blocks.share, blocks.slot

        def step(group, _):
            sets = [
                message[half, group * share + d].astype(F32)[base : base + 8]
                for d in range(share)
            ]
            pieces = [
                jnp.concatenate([s[:, g * slot : (g + 1) * slot] for s in sets], 1)
                for g in range(blocks.groups)
            ]
            at = half * blocks.half + blocks.main + group * LANES
            lay(at, jnp.concatenate(pieces, 0))
            return 0

        lax.fori_loop(0, ranks // share, step, 0)

    def hand_on(d, _):
        source = lax.rem(me + ranks - d, ranks)
        to_rank(source, source).wait_recv()
        to_pair(source, lat).start()
        return 0

    lax.fori_loop(1, ranks, hand_on, 0)

    for r in range(levels // 2, levels, 2):
        azimuth(r)

    def mine(source, _):
        lay_main(lat, source)
        return 0

    lax.fori_loop(0, ranks, mine, 0)
    lay_tails(lat)

    def theirs(source, _):
        to_pair(source, 1 - lat).wait_recv()
        lay_main(1 - lat, source)
        return 0

    lax.fori_loop(0, ranks, theirs, 0)
    lay_tails(1 - lat)

    coeffs = lax.dot_general(spread[...], hot[...], across, preferred_element_type=F32)
    lane = lax.broadcasted_iota(jnp.int32, (values, LOW), 1)

    def allowed(i, n):
        return lane + n * LOW >= modes_ref[i]

    load_legendre.wait()
    load_weight.wait()
    for i in range(modes):
        rows = []
        for n in range(chunks):
            at = (i * chunks + n) * values
            rows.append(jnp.where(allowed(i, n), coeffs[at : at + values], 0.0).astype(BF16))
        value = jnp.dot(jnp.concatenate(rows, 1), legendre[i], preferred_element_type=F32)
        value = value.astype(BF16).astype(F32)
        spectral[i] = value
        for f in range(fields):
            turned[i, f * 8 : f * 8 + 8] = pltpu.roll(value[f * 8 : f * 8 + 8], 4, 0)

    sums = []
    for j in range(modes):
        stack = []
        for f in range(fields):
            parts = []
            for part in range(cycles // LANES):
                acc = None
                for e, source in enumerate((spectral, turned)):
                    for i in range(modes):
                        at = ((e * modes + i) * 8 + j) * 8
                        term = (
                            source[i, f * 8 : f * 8 + 8, part * LANES : (part + 1) * LANES]
                            * waves[part, at : at + 8, :]
                        )
                        acc = term if acc is None else acc + term
                parts.append(acc)
            stack.append(jnp.concatenate(parts, 1))
        sums.append((jnp.concatenate(stack, 0) * weight[...][None, :]).astype(BF16))

    pieces = []
    for i in range(modes):
        value = lax.dot_general(sums[i], legendre[i], across, preferred_element_type=F32)
        for n in range(chunks):
            piece = value[:, n * LOW : (n + 1) * LOW]
            pieces.append(jnp.where(allowed(i, n), piece, 0.0))
    advection = jnp.concatenate(pieces, 0).astype(BF16)

    wide = 4 * LANES

    def collect(at):
        here = pl.ds(pl.multiple_of(at, LANES), wide)
        value = jnp.dot(advection, hot[:, here], preferred_element_type=F32)
        high = lax.shift_right_arithmetic(slots[:, here], SHIFT)
        acc = jnp.zeros((values, wide), F32)
        for h in range(high_count):
            acc = jnp.where(high == h, value[h * values : (h + 1) * values], acc)
        return acc

    def collect_half(half, handle):
        slot = blocks.slot
        many = wide // slot

        def tail_step(n, _):
            value = collect(half * blocks.half + blocks.main + n * wide)
            for d in range(many):
                tails[n * many + d] = blocks.lanes(
                    [
                        value[g * 8 : g * 8 + 8, d * slot : (d + 1) * slot]
                        for g in range(blocks.groups)
                    ]
                )
            return 0

        lax.fori_loop(0, ranks // many, tail_step, 0)

        if blocks.full:

            def main_step(n, _):
                turn = lax.rem(me // 4 + 1 + n, ranks // 4)
                value = collect(half * blocks.half + turn * wide)
                for u in range(4):
                    rank = turn * 4 + u
                    handle(
                        rank, blocks.join(value[:, u * LANES : (u + 1) * LANES], tails[rank])
                    )
                return 0

            lax.fori_loop(0, ranks // 4, main_step, 0)
        else:

            def rank_step(n, _):
                rank = lax.rem(me + 1 + n, ranks)
                handle(rank, blocks.join(None, tails[rank]))
                return 0

            lax.fori_loop(0, ranks, rank_step, 0)

    def pair_back(rank):
        return pltpu.make_async_remote_copy(
            src_ref=give.at[rank], dst_ref=other.at[rank],
            send_sem=pass2_sem.at[rank], recv_sem=got2_sem.at[rank],
            device_id=(me, 1 - lat), device_id_type=MESH,
        )

    def rank_back(rank, source):
        return pltpu.make_async_remote_copy(
            src_ref=total.at[rank], dst_ref=back.at[source],
            send_sem=send2_sem.at[rank], recv_sem=recv2_sem.at[source],
            device_id=(rank, lat), device_id_type=MESH,
        )

    def to_other(rank, block):
        give[rank] = block.astype(BF16)
        pair_back(rank).start()

    def to_owner(rank, block):
        pair_back(rank).wait_recv()
        total[rank] = (block + other[rank].astype(F32)).astype(BF16)

        @pl.when(rank != me)
        def _():
            rank_back(rank, me).start()

    keep.wait()
    collect_half(1 - lat, to_other)
    collect_half(lat, to_owner)
    back[me] = total[me]

    def sent(d, _):
        rank = lax.rem(me + d, ranks)
        to_rank(rank, me).wait_send()
        to_pair(rank, lat).wait_send()
        pair_back(rank).wait_send()
        return 0

    lax.fori_loop(1, ranks, sent, 0)
    to_pair(me, lat).wait_send()
    pair_back(me).wait_send()

    def arrived(d, _):
        source = lax.rem(me + ranks - d, ranks)
        rank_back(source, source).wait_recv()
        return 0

    lax.fori_loop(1, ranks, arrived, 0)

    def sent_back(d, _):
        rank_back(lax.rem(me + d, ranks), me).wait_send()
        return 0

    lax.fori_loop(1, ranks, sent_back, 0)


def last_kernel(
    blocks, spacing, back, solved, solved_out, out, held, solved_sem
):
    ranks, values, base = blocks.ranks, blocks.values, blocks.base
    items, depth, columns = out.shape
    levels = depth // ranks

    hand_on = pltpu.make_async_copy(solved, solved_out, solved_sem)
    hand_on.start()
    edge = 8
    held[:, 0:edge, :] = jnp.zeros((items, edge, columns), F32)
    held[:, edge + depth : 2 * edge + depth, :] = jnp.zeros((items, edge, columns), F32)
    for rank in range(ranks):
        value = back[rank].astype(F32)
        tail = jnp.concatenate(
            [
                value[base : base + 8, g * blocks.slot : g * blocks.slot + blocks.tail]
                for g in range(blocks.groups)
            ],
            0,
        )
        at = edge + rank * levels
        for item in range(items):
            here = slice(item * levels, (item + 1) * levels)
            if blocks.full:
                held[item, at : at + levels, 0:LANES] = value[here]
            held[item, at : at + levels, blocks.full * LANES : columns] = tail[here]

    keep = lax.broadcasted_iota(jnp.int32, (depth, depth), 0) == lax.broadcasted_iota(
        jnp.int32, (depth, depth), 1
    )
    scale = jnp.sum(jnp.where(keep, spacing[...][None, :], 0.0), axis=1, keepdims=True)
    for item in range(items):

        def shifted(n):
            return held[item, edge + n : edge + n + depth, :]

        slant = shifted(-2) - 8.0 * shifted(-1) + 8.0 * shifted(1) - shifted(2)
        out[item] = shifted(0) + scale * slant

    hand_on.wait()


def body(
    forcing,
    pivots,
    lower,
    upper,
    slab_modes,
    slot_of_column,
    legendre,
    cycle_weight,
    zonal_flow,
    inverse_spacing,
):
    ranks, halves = lax.axis_size("rad"), lax.axis_size("lat")
    columns, depth = forcing.shape[2], forcing.shape[3]
    modes, degrees, cycles = legendre.shape
    levels = zonal_flow.shape[0]
    items = 6
    values = items * levels
    blocks = Blocks(columns, values, ranks)
    line = (ranks, blocks.rows, LANES)
    total = halves * blocks.half
    matrices = [m.transpose(1, 2, 3, 0) for m in (pivots, lower, upper)]
    right = forcing.transpose(0, 1, 3, 2).reshape(items, depth, columns)
    sizes = [right, *matrices, zonal_flow, legendre]

    grid = jax.ShapeDtypeStruct((items, depth, columns), F32)

    solved, back = pl.pallas_call(
        functools.partial(kernel, blocks, halves),
        out_shape=(grid, jax.ShapeDtypeStruct(line, BF16)),
        in_specs=[SMEM] + [HBM] * 8,
        out_specs=(HBM, VMEM),
        scratch_shapes=[
            pltpu.VMEM((items, depth, columns), F32),
            pltpu.VMEM(slot_of_column.shape, jnp.int32),
            pltpu.VMEM(cycle_weight.shape, F32),
            pltpu.VMEM((1, total), jnp.int32),
        ]
        + [pltpu.VMEM(x.shape, x.dtype) for x in sizes]
        + [
            pltpu.VMEM((ranks, values, columns), F32),
            pltpu.VMEM(line, BF16),
            pltpu.VMEM((halves,) + line, BF16),
            pltpu.VMEM((LOW, total), BF16),
            pltpu.VMEM((modes * (degrees // LOW) * values, total), BF16),
            pltpu.VMEM((cycles // LANES, 2 * modes * 8 * 8, LANES), F32),
            pltpu.VMEM((modes, values, cycles), F32),
            pltpu.VMEM((modes, values, cycles), F32),
            pltpu.VMEM((ranks, 8, LANES), F32),
            pltpu.VMEM(line, BF16),
            pltpu.VMEM(line, BF16),
            pltpu.VMEM(line, BF16),
            pltpu.VMEM((4 * modes * 8, zonal_flow.shape[2]), BF16),
            pltpu.SemaphoreType.DMA((10,)),
        ]
        + [pltpu.SemaphoreType.DMA((ranks,))] * 8,
        compiler_params=pltpu.CompilerParams(
            vmem_limit_bytes=(54 if total <= 8000 else 60) * MIB, collective_id=0, has_side_effects=True
        ),
        name="step",
    )(slab_modes, slot_of_column, cycle_weight, right, *matrices, zonal_flow, legendre)

    solved, explicit = pl.pallas_call(
        functools.partial(last_kernel, blocks),
        out_shape=(grid, grid),
        in_specs=[VMEM] * 3,
        out_specs=(HBM, VMEM),
        scratch_shapes=[
            pltpu.VMEM((items, depth + 16, columns), F32),
            pltpu.SemaphoreType.DMA,
        ],
        compiler_params=pltpu.CompilerParams(vmem_limit_bytes=16 * MIB),
        name="stencil",
    )(inverse_spacing, back, solved)

    def placed(value):
        return value.reshape(3, 2, depth, columns).transpose(0, 1, 3, 2)

    return (placed(solved), placed(explicit))


def solution(mesh):
    placed = (
        P(None, None, ("rad", "lat"), None),
        P(("rad", "lat"), None, None, None),
        P(("rad", "lat"), None, None, None),
        P(("rad", "lat"), None, None, None),
        P(),
        P(),
        P(None, None, "lat"),
        P("lat"),
        P("rad", "lat", None),
        P(),
    )
    return jax.shard_map(
        body,
        mesh=mesh,
        in_specs=placed,
        out_specs=(P(None, None, ("rad", "lat"), None), P(None, None, ("rad", "lat"), None)),
        check_vma=False,
    )
```
